256 devices in a mesh: sib: 8 (over x_hi, y), wide: 32 (over x_lo, z, core).
Axes of the slice: x: 4 (x_hi: 2, x_lo: 2; x = x_hi * 2 + x_lo), y: 4, z: 8, core: 2. Of those that a mesh axis runs over, the one named last changes fastest.
Arguments:
- right_side: float32 [128, 32, 4096], P(None, 'wide', 'sib'), may hold values from -6 to 6
- tree_order: int32 [32, 4096], P('wide', 'sib'), may hold values from 0 to 4095, each once within a row
- x_start: float32 [128, 32, 4096], P(None, 'wide', 'sib'), may hold values from -6 to 6
- tangent_start: float32 [128, 32, 4096], P(None, 'wide', 'sib'), may hold values from -3 to 3
- dense_kernel: float32 [32, 8, 512, 512], P('wide', 'sib'), may hold values from -0.25 to 0.25
- dense_deriv: float32 [32, 8, 512, 512], P('wide', 'sib'), may hold values from -0.25 to 0.25
- leaf_basis: float32 [32, 8, 512, 256], P('wide', 'sib'), may hold values from -0.25 to 0.25
- transfer: float32 [32, 8, 256, 256], P('wide', 'sib'), may hold values from -0.375 to 0.375
- sibling_kernel: float32 [32, 8, 7, 256, 256], P('wide', 'sib'), may hold values from -0.125 to 0.125
- sibling_deriv: float32 [32, 8, 7, 256, 256], P('wide', 'sib'), may hold values from -0.125 to 0.125
- partner_list: int32 [32, 4], P('wide'), may hold values from 0 to 31, as said below
- parent_kernel: float32 [32, 4, 256, 256], P('wide'), may hold values from -0.1875 to 0.1875
- parent_deriv: float32 [32, 4, 256, 256], P('wide'), may hold values from -0.1875 to 0.1875
Outputs:
- solution: float32 [128, 32, 4096], P(None, 'wide', 'sib')
- tangent: float32 [128, 32, 4096], P(None, 'wide', 'sib')
The draws below stay inside these ranges and needn't reach their ends.
Inputs may be any that keep to these rules, and one draw needn't show every extreme that they name: `partner_list`: row p names 4 different parent clusters, none of them p. `tree_order`: each row holds every position 0 .. 4095 once.
All inputs are finite; a program needn't handle non-finite values.
Results may differ from the reference program's by a relative error of at most 0.0001.
Values sent between devices are 32-bit elements; how exact they have to be, the bound alone decides.
A program may use at most 64 MiB of HBM per device.

```python
import jax
import jax.numpy as jnp
from jax import lax

LEAF = 512
RHS = 128
RANK = 256
NB_PAR = 4
ITERS = 2
PARENTS = 32
PTS_PAR = 4096
N_SIB = 8


def draw_partner_list(key, part):
    key = jax.random.fold_in(key, 7)
    scores = jax.random.randint(key, (PARENTS, PARENTS - 1), 0, 1 << 20)
    scores = scores * PARENTS + jnp.arange(PARENTS - 1, dtype=jnp.int32)[None, :]
    chosen = lax.top_k(scores, NB_PAR)[1].astype(jnp.int32)
    rows = jnp.arange(PARENTS, dtype=jnp.int32)[:, None]
    return ((rows + chosen + 1) % PARENTS).astype(jnp.int32)


def block_scale(stream_key, dims, split, low, high):
    def one(dim, parts):
        draws = jax.random.uniform(jax.random.fold_in(jax.random.fold_in(stream_key, 6), dim), (parts,), jnp.float32, low / len(split), high / len(split))
        return jnp.repeat(jnp.exp(draws), dims[dim] // parts).reshape((-1,) + (1,) * (len(dims) - dim - 1))

    loudness = one(*split[0])
    for cut in split[1:]:
        loudness = loudness * one(*cut)
    return loudness


def normal_values(key, extent, scale, most, shards=(), kind=jnp.bfloat16):
    result = jax.random.normal(key, extent, jnp.float32) * scale
    if len(shards) > 0:
        result = block_scale(key, extent, shards, -0.22, 0.18) * result
    return jnp.clip(result, min=-most, max=most).astype(kind)


def setup_inputs(seed: int = 0) -> dict:
    keys = jax.random.split(jax.random.key(seed), 14)
    return {
        "right_side": normal_values(keys[0], (RHS, PARENTS, PTS_PAR), 1.0, 6.0, ((1, 32), (2, 8)), jnp.float32),
        "tree_order": jax.vmap(lambda own: jax.random.permutation(own, PTS_PAR))(jax.random.split(keys[1], PARENTS)).reshape((PARENTS, PTS_PAR)).astype(jnp.int32),
        "x_start": normal_values(keys[2], (RHS, PARENTS, PTS_PAR), 1.0, 6.0, ((1, 32), (2, 8)), jnp.float32),
        "tangent_start": normal_values(keys[3], (RHS, PARENTS, PTS_PAR), 0.5, 3.0, ((1, 32), (2, 8)), jnp.float32),
        "dense_kernel": normal_values(keys[4], (PARENTS, N_SIB, LEAF, LEAF), LEAF ** -0.5, 0.25, ((0, 32), (1, 8)), jnp.float32),
        "dense_deriv": normal_values(keys[5], (PARENTS, N_SIB, LEAF, LEAF), LEAF ** -0.5, 0.25, ((0, 32), (1, 8)), jnp.float32),
        "leaf_basis": normal_values(keys[6], (PARENTS, N_SIB, LEAF, RANK), LEAF ** -0.5, 0.25, ((0, 32), (1, 8)), jnp.float32),
        "transfer": normal_values(keys[7], (PARENTS, N_SIB, RANK, RANK), RANK ** -0.5, 0.375, ((0, 32), (1, 8)), jnp.float32),
        "sibling_kernel": normal_values(keys[8], (PARENTS, N_SIB, N_SIB - 1, RANK, RANK), (RANK * (N_SIB - 1)) ** -0.5, 0.125, ((0, 32), (1, 8)), jnp.float32),
        "sibling_deriv": normal_values(keys[9], (PARENTS, N_SIB, N_SIB - 1, RANK, RANK), (RANK * (N_SIB - 1)) ** -0.5, 0.125, ((0, 32), (1, 8)), jnp.float32),
        "partner_list": draw_partner_list(jax.random.fold_in(keys[13], 71), 0),
        "parent_kernel": normal_values(keys[11], (PARENTS, NB_PAR, RANK, RANK), (RANK * NB_PAR) ** -0.5, 0.1875, ((0, 32),), jnp.float32),
        "parent_deriv": normal_values(keys[12], (PARENTS, NB_PAR, RANK, RANK), (RANK * NB_PAR) ** -0.5, 0.1875, ((0, 32),), jnp.float32),
    }


highest = lax.Precision.HIGHEST
relax_step = 0.3
noise_level = 1.0


def contract(form, left, right):
    return jnp.einsum(form, left, right, precision=highest, preferred_element_type=jnp.float32)


def siblings(coeff, couple):
    total = jnp.zeros_like(coeff)
    for offset in range(1, N_SIB):
        total = total + contract('rpsk,pskm->rpsm', jnp.roll(coeff, -offset, axis=2), couple[:, :, offset - 1])
    return total


def reference(right_side, tree_order, x_start, tangent_start, dense_kernel, dense_deriv, leaf_basis, transfer, sibling_kernel, sibling_deriv, partner_list, parent_kernel, parent_deriv):
    shape = (RHS, PARENTS, N_SIB, LEAF)
    order = jnp.broadcast_to(tree_order[None].astype(jnp.int32), right_side.shape)
    rhs = jnp.take_along_axis(right_side, order, axis=2).reshape(shape)
    x = x_start.reshape(shape)
    dx = tangent_start.reshape(shape)
    for step in range(ITERS):
        ax = contract('rpsl,pslk->rpsk', x, leaf_basis)
        adx = contract('rpsl,pslk->rpsk', dx, leaf_basis)
        gx = siblings(ax, sibling_kernel)
        gdx = siblings(ax, sibling_deriv) + siblings(adx, sibling_kernel)
        px = contract('rpsk,pskm->rpm', ax, transfer)
        pdx = contract('rpsk,pskm->rpm', adx, transfer)
        cx = jnp.take(px, partner_list.astype(jnp.int32), axis=1)
        cdx = jnp.take(pdx, partner_list.astype(jnp.int32), axis=1)
        hx = contract('rpbk,pbkm->rpm', cx, parent_kernel)
        hdx = contract('rpbk,pbkm->rpm', cx, parent_deriv) + contract('rpbk,pbkm->rpm', cdx, parent_kernel)
        zx = gx + contract('rpm,pskm->rpsk', hx, transfer)
        zdx = gdx + contract('rpm,pskm->rpsk', hdx, transfer)
        image = contract('rpsl,pslm->rpsm', x, dense_kernel) + contract('rpsk,pslk->rpsl', zx, leaf_basis)
        dimage = (contract('rpsl,pslm->rpsm', x, dense_deriv) + contract('rpsl,pslm->rpsm', dx, dense_kernel)
                  + contract('rpsk,pslk->rpsl', zdx, leaf_basis))
        x_next = x + relax_step * (rhs - noise_level * x - image)
        dx = dx - relax_step * (noise_level * dx + dimage)
        x = x_next
    return x.reshape(RHS, PARENTS, PTS_PAR), dx.reshape(RHS, PARENTS, PTS_PAR)
```

```python
import functools

import jax
import jax.numpy as jnp
from jax import lax
from jax.experimental import pallas as pl
from jax.experimental.pallas import tpu as pltpu
from jax.sharding import PartitionSpec as P

ITERS = 2
N_SIB = 8
N_Z = 8
LEAF = 512
RHS = 128
RANK = 256
NB_PAR = 4
PARENTS = 32
ROWS = RHS // N_SIB
LANES = 128

relax_step = 0.3
noise_level = 1.0

f32 = jnp.float32
bf16 = jnp.bfloat16
MESH = pl.DeviceIdType.MESH

SIB_ORDER = (1, 7, 4, 3, 5, 2, 6)
Z_ORDER = (0, 1, 7, 2, 6, 3, 5, 4)


def parts(v):
    high = v.astype(bf16)
    return high, (v - high.astype(f32)).astype(bf16)


def dot(left, right):
    return jnp.dot(left, right, preferred_element_type=f32)


def dot_t(left, right):
    return lax.dot_general(left, right, (((1,), (1,)), ((), ())), preferred_element_type=f32)


def product(left, right, op=dot):
    lh, ll = left
    rh, rl = right
    rows = lh.shape[0]
    both = op(jnp.concatenate([lh, ll], axis=0), rh)
    return both[:rows] + (both[rows:] + op(lh, rl))


def kernel(
    rhs_hbm, order_hbm, x_hbm, dx_hbm, dense_hbm, dense_d_hbm, basis_hbm, trans_hbm, sib_k_hbm, sib_d_hbm,
    partners, par_k_hbm, par_d_hbm,
    x_out, dx_out,
    x_in, dx_in, dense_in, dense_d_in, basis_in, trans_in, sib_k_in, sib_d_in, par_k_in, par_d_in,
    dense_h, dense_l, dense_d_h, dense_d_l, basis_h, basis_l, trans_h, trans_l,
    sib_k_h, sib_k_l, sib_d_h, sib_d_l, par_k_h, par_k_l, par_d_h, par_d_l,
    state, coeff, coeff_in, term, term_in, upper_0, upper_1, field,
    points_in, points, order, placed, rhs,
    load_sem, coeff_s, coeff_r, term_s, term_r, field_s, field_r,
    z_s, z_r, xlo_s, xlo_r, core_s, core_r, rhs_s, rhs_r, order_s, order_r, back_s, back_r,
):
    me = lax.axis_index("sib")
    wide = lax.axis_index("wide")
    xlo, z, core = wide // 16, wide // 2 % N_Z, wide % 2

    def sib_at(o):
        return lax.rem(me + o, N_SIB)

    def sib_dev(o):
        return (sib_at(o), wide)

    def parent(xl, zz, cc):
        return xl * 16 + lax.rem(zz + N_Z, N_Z) * 2 + cc

    loads = {}

    def load(name, src, dst, k):
        loads[name] = pltpu.make_async_copy(src, dst, load_sem.at[k])
        loads[name].start()

    load("x", x_hbm, x_in, 0)
    load("basis", basis_hbm.at[0, 0], basis_in, 1)
    load("dx", dx_hbm, dx_in, 2)
    load("trans", trans_hbm.at[0, 0], trans_in, 3)
    load("points", rhs_hbm.at[pl.ds(pl.multiple_of(me * ROWS, ROWS), ROWS)], points_in.at[me], 4)
    load("order", order_hbm, order.at[me], 5)
    load("dense", dense_hbm.at[0, 0], dense_in, 6)
    load("dense_d", dense_d_hbm.at[0, 0], dense_d_in, 7)
    load("par_k", par_k_hbm.at[0], par_k_in, 8)
    load("par_d", par_d_hbm.at[0], par_d_in, 9)
    load("sib_k", sib_k_hbm.at[0, 0], sib_k_in, 10)
    load("sib_d", sib_d_hbm.at[0, 0], sib_d_in, 11)

    barrier = pltpu.get_barrier_semaphore()

    def greet(device):
        pl.semaphore_signal(barrier, inc=1, device_id=device, device_id_type=MESH)

    for o in range(1, N_SIB):
        greet(sib_dev(o))
    for d in range(1, N_Z):
        greet((me, parent(xlo, z + d, core)))
    greet((me, parent(1 - xlo, z, core)))
    greet((me, parent(xlo, z, 1 - core)))

    sent = []

    def send(src, dst, ssem, rsem, device):
        c = pltpu.make_async_remote_copy(
            src_ref=src, dst_ref=dst, send_sem=ssem, recv_sem=rsem, device_id=device, device_id_type=MESH
        )
        c.start()
        sent.append(c)
        return c

    def split(src, high, low):
        h, l = parts(src)
        high[...] = h
        low[...] = l

    def coefficients(it):
        v = parts(state[it])
        c = product(v, (basis_h[...], basis_l[...]))
        coeff[it] = c
        t = product(parts(c), (trans_h[...], trans_l[...]))
        for s in range(N_SIB):
            term[it, s, :ROWS] = t[s * ROWS:(s + 1) * ROWS]
            term[it, s, ROWS:] = t[RHS + s * ROWS:RHS + (s + 1) * ROWS]

    loads["x"].wait()
    state[0, :RHS] = x_in[...].reshape(RHS, LEAF)
    loads["basis"].wait()
    split(basis_in[...], basis_h, basis_l)
    loads["dx"].wait()
    state[0, RHS:] = dx_in[...].reshape(RHS, LEAF)
    loads["trans"].wait()
    split(trans_in[...], trans_h, trans_l)
    coefficients(0)

    pl.semaphore_wait(barrier, 7 + 7 + 2)

    for it in range(ITERS):
        last = it == ITERS - 1
        upper = (upper_0, upper_1)[it]
        for o in SIB_ORDER:
            send(term.at[it, sib_at(o)], term_in.at[it, o - 1], term_s.at[it, o - 1], term_r.at[it, o - 1], sib_dev(o))
        if it == 0:
            loads["points"].wait()
            loads["order"].wait()
            for o in SIB_ORDER:
                send(order.at[me], order.at[me], order_s.at[o - 1], order_r.at[o - 1], sib_dev(o))
                send(
                    rhs_hbm.at[pl.ds(pl.multiple_of(sib_at(o) * ROWS, ROWS), ROWS)], points_in.at[me],
                    rhs_s.at[o - 1], rhs_r.at[o - 1], sib_dev(o),
                )
        for o in SIB_ORDER:
            send(
                coeff.at[it], coeff_in.at[it, o - 1], coeff_s.at[it, o - 1], coeff_r.at[it, o - 1],
                sib_dev(N_SIB - o),
            )

        def arrived(buf, sem):
            pltpu.make_async_copy(buf, buf, sem).wait()

        if it == 0:
            loads["dense"].wait()
            split(dense_in[...], dense_h, dense_l)
            loads["dense_d"].wait()
            split(dense_d_in[...], dense_d_h, dense_d_l)
        vh, vl = parts(state[it])
        own = product((vh, vl), (dense_h[...], dense_l[...]))
        own_d = product((vh[:RHS], vl[:RHS]), (dense_d_h[...], dense_d_l[...]))
        state[it + 1, :RHS] = own[:RHS]
        state[it + 1, RHS:] = own[RHS:] + own_d

        total = term[it, me]
        for o in SIB_ORDER:
            arrived(term_in.at[it, o - 1], term_r.at[it, o - 1])
            total = total + term_in[it, o - 1]
        upper[wide] = total

        def to_xlo(d):
            at = parent(xlo, z - d, core)
            send(upper.at[at], upper.at[at], xlo_s.at[it, d], xlo_r.at[it, d], (me, parent(1 - xlo, z, core)))

        def to_core(xl, far, d):
            at = parent(xl, z - d, core)
            send(
                upper.at[at], upper.at[at], core_s.at[it, far * N_Z + d], core_r.at[it, far * N_Z + d],
                (me, parent(xlo, z, 1 - core)),
            )

        for d in Z_ORDER[1:]:
            send(
                upper.at[wide], upper.at[wide], z_s.at[it, d - 1], z_r.at[it, d - 1],
                (me, parent(xlo, z + d, core)),
            )
        to_xlo(0)
        to_core(xlo, 0, 0)

        if it == 0:
            loads["par_k"].wait()
            split(par_k_in[...], par_k_h, par_k_l)
            loads["par_d"].wait()
            split(par_d_in[...], par_d_h, par_d_l)
            loads["sib_k"].wait()
            loads["sib_d"].wait()

            for o in SIB_ORDER:
                arrived(order.at[sib_at(o)], order_r.at[N_SIB - o - 1])
                arrived(points_in.at[sib_at(o)], rhs_r.at[N_SIB - o - 1])
            for s in range(N_SIB):
                seg = points_in[s].reshape(ROWS, LEAF)
                for q in range(LEAF // LANES):
                    points[s * (LEAF // LANES) + q] = seg[:, q * LANES:(q + 1) * LANES]

            def place(s, _):
                want_all = order[s]
                for q in range(LEAF // LANES):
                    want = jnp.broadcast_to(want_all[:, q * LANES:(q + 1) * LANES], (ROWS, LANES))
                    block = want // LANES
                    lane = want % LANES
                    got = jnp.zeros((ROWS, LANES), f32)
                    for b in range(PARENTS):
                        found = jnp.take_along_axis(points[b], lane, axis=1, mode="promise_in_bounds")
                        got = jnp.where(block == b, found, got)
                    placed[s, :, q * LANES:(q + 1) * LANES] = got
                return 0

            lax.fori_loop(0, N_SIB, place, 0)
            rhs[me] = placed[me]
            for o in SIB_ORDER:
                send(placed.at[sib_at(o)], rhs.at[me], back_s.at[o - 1], back_r.at[o - 1], sib_dev(o))

        def from_z(d):
            if d:
                at = upper.at[parent(xlo, z - d, core)]
                arrived(at, z_r.at[it, d - 1])
                to_xlo(d)
                to_core(xlo, 0, d)

        def from_xlo(d):
            arrived(upper.at[parent(1 - xlo, z - d, core)], xlo_r.at[it, d])
            to_core(1 - xlo, 1, d)

        for k in range(N_Z + 2):
            if k < N_Z:
                from_z(Z_ORDER[k])
            if k >= 2:
                from_xlo(Z_ORDER[k - 2])
        for far in range(2):
            for d in Z_ORDER:
                arrived(
                    upper.at[parent(far + xlo - 2 * far * xlo, z - d, 1 - core)], core_r.at[it, far * N_Z + d]
                )

        hx = jnp.zeros((ROWS, RANK), f32)
        hd = jnp.zeros((ROWS, RANK), f32)
        for k in range(NB_PAR):
            ch, cl = parts(upper[partners[0, k]])
            kk = product((ch, cl), (par_k_h[k], par_k_l[k]))
            kd = product((ch[:ROWS], cl[:ROWS]), (par_d_h[k], par_d_l[k]))
            hx = hx + kk[:ROWS]
            hd = hd + (kk[ROWS:] + kd)
        field[it, me, :ROWS] = hx
        field[it, me, ROWS:] = hd
        for o in SIB_ORDER:
            send(field.at[it, me], field.at[it, me], field_s.at[it, o - 1], field_r.at[it, o - 1], sib_dev(o))

        gx = jnp.zeros((2 * RHS, RANK), f32)
        gd = jnp.zeros((RHS, RANK), f32)
        for o in SIB_ORDER:
            if it == 0:
                split(sib_k_in[o - 1], sib_k_h.at[o - 1], sib_k_l.at[o - 1])
                split(sib_d_in[o - 1], sib_d_h.at[o - 1], sib_d_l.at[o - 1])
            arrived(coeff_in.at[it, o - 1], coeff_r.at[it, o - 1])
            ah, al = parts(coeff_in[it, o - 1])
            gx = gx + product((ah, al), (sib_k_h[o - 1], sib_k_l[o - 1]))
            gd = gd + product((ah[:RHS], al[:RHS]), (sib_d_h[o - 1], sib_d_l[o - 1]))

        for o in SIB_ORDER:
            arrived(field.at[it, sib_at(o)], field_r.at[it, N_SIB - o - 1])
        h = jnp.concatenate(
            [field[it, :, :ROWS].reshape(RHS, RANK), field[it, :, ROWS:].reshape(RHS, RANK)], axis=0
        )
        down = product(parts(h), (trans_h[...], trans_l[...]), dot_t) + gx
        down = jnp.concatenate([down[:RHS], down[RHS:] + gd], axis=0)
        image = state[it + 1] + product(parts(down), (basis_h[...], basis_l[...]), dot_t)
        if it == 0:
            for o in SIB_ORDER:
                arrived(rhs.at[sib_at(o)], back_r.at[N_SIB - o - 1])
        x = state[it, :RHS]
        dx = state[it, RHS:]
        x_next = x + relax_step * (rhs[...].reshape(RHS, LEAF) - noise_level * x - image[:RHS])
        dx_next = dx - relax_step * (noise_level * dx + image[RHS:])
        if last:
            x_out[...] = x_next.reshape(RHS, 1, LEAF)
            dx_out[...] = dx_next.reshape(RHS, 1, LEAF)
        else:
            state[it + 1, :RHS] = x_next
            state[it + 1, RHS:] = dx_next
            coefficients(it + 1)

    for c in sent:
        c.wait_send()


def body(*args):
    V = pltpu.VMEM
    D = pltpu.SemaphoreType.DMA
    any_space = pl.BlockSpec(memory_space=pl.ANY)
    specs = [any_space] * 13
    specs[10] = pl.BlockSpec(memory_space=pltpu.SMEM)
    out = jax.ShapeDtypeStruct((RHS, 1, LEAF), f32)
    weights = [(LEAF, LEAF)] * 2 + [(LEAF, RANK), (RANK, RANK)] + [(N_SIB - 1, RANK, RANK)] * 2 + [(NB_PAR, RANK, RANK)] * 2
    scratch = [V((RHS, 1, LEAF), f32)] * 2
    scratch += [V(w, f32) for w in weights]
    for w in weights:
        scratch += [V(w, bf16)] * 2
    scratch += [
        V((ITERS + 1, 2 * RHS, LEAF), f32),
        V((ITERS, 2 * RHS, RANK), f32),
        V((ITERS, N_SIB - 1, 2 * RHS, RANK), f32),
        V((ITERS, N_SIB, 2 * ROWS, RANK), f32),
        V((ITERS, N_SIB - 1, 2 * ROWS, RANK), f32),
        V((PARENTS, 2 * ROWS, RANK), f32),
        V((PARENTS, 2 * ROWS, RANK), f32),
        V((ITERS, N_SIB, 2 * ROWS, RANK), f32),
        V((N_SIB, ROWS, 1, LEAF), f32),
        V((PARENTS, ROWS, LANES), f32),
        V((N_SIB, 1, LEAF), jnp.int32),
        V((N_SIB, ROWS, LEAF), f32),
        V((N_SIB, ROWS, LEAF), f32),
        D((12,)),
    ]
    peers = N_SIB - 1
    scratch += [D((ITERS, peers))] * 6
    scratch += [D((ITERS, N_Z - 1))] * 2 + [D((ITERS, N_Z))] * 2 + [D((ITERS, 2 * N_Z))] * 2
    scratch += [D((peers,))] * 6
    return pl.pallas_call(
        kernel,
        out_shape=(out, out),
        in_specs=specs,
        out_specs=(pl.BlockSpec(memory_space=pltpu.VMEM), pl.BlockSpec(memory_space=pltpu.VMEM)),
        scratch_shapes=scratch,
        compiler_params=pltpu.CompilerParams(
            collective_id=0, has_side_effects=True, vmem_limit_bytes=52 * 1024 * 1024
        ),
        name="richardson",
    )(*args)


def solution(mesh):
    placed = (
        P(None, "wide", "sib"),
        P("wide", "sib"),
        P(None, "wide", "sib"),
        P(None, "wide", "sib"),
        P("wide", "sib", None, None),
        P("wide", "sib", None, None),
        P("wide", "sib", None, None),
        P("wide", "sib", None, None),
        P("wide", "sib", None, None, None),
        P("wide", "sib", None, None, None),
        P("wide", None),
        P("wide", None, None, None),
        P("wide", None, None, None),
    )
    return jax.shard_map(
        body,
        mesh=mesh,
        in_specs=placed,
        out_specs=(P(None, "wide", "sib"), P(None, "wide", "sib")),
        check_vma=False,
    )
```

```python
import functools

import jax
import jax.numpy as jnp
from jax import lax
from jax.experimental import pallas as pl
from jax.experimental.pallas import tpu as pltpu
from jax.sharding import PartitionSpec as P

ITERS = 2
N_SIB = 8
N_Z = 8
LEAF = 512
RHS = 128
RANK = 256
NB_PAR = 4
PARENTS = 32
ROWS = RHS // N_SIB
LANES = 128

relax_step = 0.3
noise_level = 1.0

f32 = jnp.float32
bf16 = jnp.bfloat16
MESH = pl.DeviceIdType.MESH

SIB_ORDER = (1, 7, 4, 3, 5, 2, 6)
BLOCKS = ((1, 0), (0, -1), (0, 1), (1, -1), (1, 1), (0, 2), (1, 2))
Z_ORDER = (0, 1, 7, 2, 6, 3, 5, 4)


def parts(v):
    high = v.astype(bf16)
    return high, (v - high.astype(f32)).astype(bf16)


def dot(left, right):
    return jnp.dot(left, right, preferred_element_type=f32)


def dot_t(left, right):
    return lax.dot_general(left, right, (((1,), (1,)), ((), ())), preferred_element_type=f32)


def product(left, right, op=dot):
    lh, ll = left
    rh, rl = right
    rows = lh.shape[0]
    both = op(jnp.concatenate([lh, ll], axis=0), rh)
    return both[:rows] + (both[rows:] + op(lh, rl))


def kernel(
    rhs_hbm, order_hbm, x_hbm, dx_hbm, dense_hbm, dense_d_hbm, basis_hbm, trans_hbm, sib_k_hbm, sib_d_hbm,
    partners_hbm, par_k_hbm, par_d_hbm,
    x_out, dx_out,
    x_in, dx_in, dense_in, dense_d_in, basis_in, trans_in, sib_k_in, sib_d_in, par_k_in, par_d_in,
    dense_h, dense_l, dense_d_h, dense_d_l, basis_h, basis_l, trans_h, trans_l,
    sib_k_h, sib_k_l, sib_d_h, sib_d_l, par_k_h, par_k_l, par_d_h, par_d_l,
    state, coeff, coeff_in, term, term_in, upper_0, upper_1, field,
    points_in, points, order, placed, rhs, partners,
    load_sem, coeff_s, coeff_r, term_s, term_r, field_s, field_r,
    z_s, z_r, xlo_s, xlo_r, core_s, core_r, rhs_s, rhs_r, order_s, order_r, back_s, back_r,
):
    me = lax.axis_index("sib")
    wide = lax.axis_index("wide")
    xlo, z, core = wide // 16, wide // 2 % N_Z, wide % 2

    def sib_at(o):
        return lax.rem(me + o, N_SIB)

    def sib_dev(o):
        return (sib_at(o), wide)

    xhi, y = me // 4, me % 4

    def near(dx, dy):
        return lax.rem(xhi + dx, 2) * 4 + lax.rem(y + dy + 4, 4)

    across, y_next, y_prev = (near(1, 0), wide), (near(0, 1), wide), (near(0, -1), wide)

    def parent(xl, zz, cc):
        return xl * 16 + lax.rem(zz + N_Z, N_Z) * 2 + cc

    loads = {}

    def load(name, src, dst, k):
        loads[name] = pltpu.make_async_copy(src, dst, load_sem.at[k])
        loads[name].start()

    load("x", x_hbm, x_in, 0)
    load("basis", basis_hbm.at[0, 0], basis_in, 1)
    load("dx", dx_hbm, dx_in, 2)
    load("trans", trans_hbm.at[0, 0], trans_in, 3)
    load("points", rhs_hbm.at[pl.ds(pl.multiple_of(me * ROWS, ROWS), ROWS)], points_in.at[me], 4)
    load("order", order_hbm, order.at[me], 5)
    load("dense", dense_hbm.at[0, 0], dense_in, 6)
    load("dense_d", dense_d_hbm.at[0, 0], dense_d_in, 7)
    load("partners", partners_hbm, partners, 12)
    load("par_k", par_k_hbm.at[0], par_k_in, 8)
    load("par_d", par_d_hbm.at[0], par_d_in, 9)
    load("sib_k", sib_k_hbm.at[0, 0], sib_k_in, 10)
    load("sib_d", sib_d_hbm.at[0, 0], sib_d_in, 11)

    barrier = pltpu.get_barrier_semaphore()

    def greet(device):
        pl.semaphore_signal(barrier, inc=1, device_id=device, device_id_type=MESH)

    for o in range(1, N_SIB):
        greet(sib_dev(o))
    for d in range(1, N_Z):
        greet((me, parent(xlo, z + d, core)))
    greet((me, parent(1 - xlo, z, core)))
    greet((me, parent(xlo, z, 1 - core)))

    sent = []

    def send(src, dst, ssem, rsem, device):
        c = pltpu.make_async_remote_copy(
            src_ref=src, dst_ref=dst, send_sem=ssem, recv_sem=rsem, device_id=device, device_id_type=MESH
        )
        c.start()
        sent.append(c)
        return c

    def arrived(buf, sem):
        pltpu.make_async_copy(buf, buf, sem).wait()

    def slot(dx, dy):
        return dx % 2 * 4 + dy % 4

    def split(src, high, low):
        h, l = parts(src)
        high[...] = h
        low[...] = l

    def coefficients(it):
        v = parts(state[it])
        c = product(v, (basis_h[...], basis_l[...]))
        coeff[it] = c
        t = product(parts(c), (trans_h[...], trans_l[...]))
        for s in range(N_SIB):
            term[it, s, :ROWS] = t[s * ROWS:(s + 1) * ROWS]
            term[it, s, ROWS:] = t[RHS + s * ROWS:RHS + (s + 1) * ROWS]

    loads["x"].wait()
    state[0, :RHS] = x_in[...].reshape(RHS, LEAF)
    loads["basis"].wait()
    split(basis_in[...], basis_h, basis_l)
    loads["dx"].wait()
    state[0, RHS:] = dx_in[...].reshape(RHS, LEAF)
    loads["trans"].wait()
    split(trans_in[...], trans_h, trans_l)
    coefficients(0)

    pl.semaphore_wait(barrier, 7 + 7 + 2)

    for it in range(ITERS):
        last = it == ITERS - 1
        upper = (upper_0, upper_1)[it]
        for o in SIB_ORDER:
            send(term.at[it, sib_at(o)], term_in.at[it, o - 1], term_s.at[it, o - 1], term_r.at[it, o - 1], sib_dev(o))
        if it == 0:
            loads["points"].wait()
            loads["order"].wait()
            for o in SIB_ORDER:
                send(order.at[me], order.at[me], order_s.at[o - 1], order_r.at[o - 1], sib_dev(o))
                send(
                    rhs_hbm.at[pl.ds(pl.multiple_of(sib_at(o) * ROWS, ROWS), ROWS)], points_in.at[me],
                    rhs_s.at[o - 1], rhs_r.at[o - 1], sib_dev(o),
                )
        gathered = []

        def piece(dx, dy, half):
            return coeff_in.at[it, slot(dx, dy), pl.ds(half * RHS, RHS)]

        def pass_on(src, dx, dy, half, device):
            send(src, piece(dx, dy, half), coeff_s.at[it, len(gathered)], coeff_r.at[it, slot(dx, dy), half], device)
            gathered.append(None)

        def have(dx, dy, half):
            arrived(piece(dx, dy, half), coeff_r.at[it, slot(dx, dy), half])

        for half in range(2):
            mine = coeff.at[it, pl.ds(half * RHS, RHS)]
            pass_on(mine, 1, 0, half, across)
            pass_on(mine, 0, -1, half, y_next)
            pass_on(mine, 0, 1, half, y_prev)

        if it == 0:
            loads["dense"].wait()
            split(dense_in[...], dense_h, dense_l)
            loads["dense_d"].wait()
            split(dense_d_in[...], dense_d_h, dense_d_l)
        vh, vl = parts(state[it])
        own = product((vh, vl), (dense_h[...], dense_l[...]))
        own_d = product((vh[:RHS], vl[:RHS]), (dense_d_h[...], dense_d_l[...]))
        state[it + 1, :RHS] = own[:RHS]
        state[it + 1, RHS:] = own[RHS:] + own_d

        total = term[it, me]
        for o in SIB_ORDER:
            arrived(term_in.at[it, o - 1], term_r.at[it, o - 1])
            total = total + term_in[it, o - 1]
        upper[wide] = total

        def to_xlo(d):
            at = parent(xlo, z - d, core)
            send(upper.at[at], upper.at[at], xlo_s.at[it, d], xlo_r.at[it, d], (me, parent(1 - xlo, z, core)))

        def to_core(xl, far, d):
            at = parent(xl, z - d, core)
            send(
                upper.at[at], upper.at[at], core_s.at[it, far * N_Z + d], core_r.at[it, far * N_Z + d],
                (me, parent(xlo, z, 1 - core)),
            )

        for d in Z_ORDER[1:]:
            send(
                upper.at[wide], upper.at[wide], z_s.at[it, d - 1], z_r.at[it, d - 1],
                (me, parent(xlo, z + d, core)),
            )
        to_xlo(0)
        to_core(xlo, 0, 0)

        for half in range(2):
            have(1, 0, half)
            pass_on(piece(1, 0, half), 1, -1, half, y_next)
            pass_on(piece(1, 0, half), 1, 1, half, y_prev)

        if it == 0:
            loads["par_k"].wait()
            split(par_k_in[...], par_k_h, par_k_l)
            loads["par_d"].wait()
            split(par_d_in[...], par_d_h, par_d_l)
            loads["sib_k"].wait()
            loads["sib_d"].wait()
            for k in range(N_SIB - 1):
                split(sib_k_in[k], sib_k_h.at[k], sib_k_l.at[k])
                split(sib_d_in[k], sib_d_h.at[k], sib_d_l.at[k])

            for o in SIB_ORDER:
                arrived(order.at[sib_at(o)], order_r.at[N_SIB - o - 1])
                arrived(points_in.at[sib_at(o)], rhs_r.at[N_SIB - o - 1])
            for s in range(N_SIB):
                seg = points_in[s].reshape(ROWS, LEAF)
                for q in range(LEAF // LANES):
                    points[s * (LEAF // LANES) + q] = seg[:, q * LANES:(q + 1) * LANES]

            def place(s, _):
                want_all = order[s]
                for q in range(LEAF // LANES):
                    want = jnp.broadcast_to(want_all[:, q * LANES:(q + 1) * LANES], (ROWS, LANES))
                    block = want // LANES
                    lane = want % LANES
                    got = jnp.zeros((ROWS, LANES), f32)
                    for b in range(PARENTS):
                        found = jnp.take_along_axis(points[b], lane, axis=1, mode="promise_in_bounds")
                        got = jnp.where(block == b, found, got)
                    placed[s, :, q * LANES:(q + 1) * LANES] = got
                return 0

            lax.fori_loop(0, N_SIB, place, 0)
            rhs[me] = placed[me]
            for o in SIB_ORDER:
                send(placed.at[sib_at(o)], rhs.at[me], back_s.at[o - 1], back_r.at[o - 1], sib_dev(o))

        def from_z(d):
            if d:
                at = upper.at[parent(xlo, z - d, core)]
                arrived(at, z_r.at[it, d - 1])
                to_xlo(d)
                to_core(xlo, 0, d)

        def from_xlo(d):
            arrived(upper.at[parent(1 - xlo, z - d, core)], xlo_r.at[it, d])
            to_core(1 - xlo, 1, d)

        def opposite(dx):
            have(dx, -1, 0)
            pass_on(piece(dx, -1, 0), dx, 2, 0, y_next)
            have(dx, 1, 1)
            pass_on(piece(dx, 1, 1), dx, 2, 1, y_prev)

        for k in range(N_Z + 2):
            if k < N_Z:
                from_z(Z_ORDER[k])
            if k == 3:
                opposite(0)
            if k >= 2:
                from_xlo(Z_ORDER[k - 2])
        opposite(1)
        for far in range(2):
            for d in Z_ORDER:
                arrived(
                    upper.at[parent(far + xlo - 2 * far * xlo, z - d, 1 - core)], core_r.at[it, far * N_Z + d]
                )

        if it == 0:
            loads["partners"].wait()
        hx = jnp.zeros((ROWS, RANK), f32)
        hd = jnp.zeros((ROWS, RANK), f32)
        for k in range(NB_PAR):
            ch, cl = parts(upper[partners[0, k]])
            kk = product((ch, cl), (par_k_h[k], par_k_l[k]))
            kd = product((ch[:ROWS], cl[:ROWS]), (par_d_h[k], par_d_l[k]))
            hx = hx + kk[:ROWS]
            hd = hd + (kk[ROWS:] + kd)
        field[it, me, :ROWS] = hx
        field[it, me, ROWS:] = hd
        for o in SIB_ORDER:
            send(field.at[it, me], field.at[it, me], field_s.at[it, o - 1], field_r.at[it, o - 1], sib_dev(o))

        gx = jnp.zeros((2 * RHS, RANK), f32)
        gd = jnp.zeros((RHS, RANK), f32)
        for dx, dy in BLOCKS:
            for half in range(2):
                if dy == 2 or dy == 1 and half == 0 or dy == -1 and half == 1:
                    have(dx, dy, half)
            at = lax.rem(near(dx, dy) - me + N_SIB, N_SIB) - 1
            ah, al = parts(coeff_in[it, slot(dx, dy)])
            gx = gx + product((ah, al), (sib_k_h[at], sib_k_l[at]))
            gd = gd + product((ah[:RHS], al[:RHS]), (sib_d_h[at], sib_d_l[at]))

        for o in SIB_ORDER:
            arrived(field.at[it, sib_at(o)], field_r.at[it, N_SIB - o - 1])
        h = jnp.concatenate(
            [field[it, :, :ROWS].reshape(RHS, RANK), field[it, :, ROWS:].reshape(RHS, RANK)], axis=0
        )
        down = product(parts(h), (trans_h[...], trans_l[...]), dot_t) + gx
        down = jnp.concatenate([down[:RHS], down[RHS:] + gd], axis=0)
        image = state[it + 1] + product(parts(down), (basis_h[...], basis_l[...]), dot_t)
        if it == 0:
            for o in SIB_ORDER:
                arrived(rhs.at[sib_at(o)], back_r.at[N_SIB - o - 1])
        x = state[it, :RHS]
        dx = state[it, RHS:]
        x_next = x + relax_step * (rhs[...].reshape(RHS, LEAF) - noise_level * x - image[:RHS])
        dx_next = dx - relax_step * (noise_level * dx + image[RHS:])
        if last:
            x_out[...] = x_next.reshape(RHS, 1, LEAF)
            dx_out[...] = dx_next.reshape(RHS, 1, LEAF)
        else:
            state[it + 1, :RHS] = x_next
            state[it + 1, RHS:] = dx_next
            coefficients(it + 1)

    for c in sent:
        c.wait_send()


def body(*args):
    V = pltpu.VMEM
    D = pltpu.SemaphoreType.DMA
    specs = [pl.BlockSpec(memory_space=pltpu.HBM)] * 13
    out = jax.ShapeDtypeStruct((RHS, 1, LEAF), f32)
    weights = [(LEAF, LEAF)] * 2 + [(LEAF, RANK), (RANK, RANK)] + [(N_SIB - 1, RANK, RANK)] * 2 + [(NB_PAR, RANK, RANK)] * 2
    scratch = [V((RHS, 1, LEAF), f32)] * 2
    scratch += [V(w, f32) for w in weights]
    for w in weights:
        scratch += [V(w, bf16)] * 2
    scratch += [
        V((ITERS + 1, 2 * RHS, LEAF), f32),
        V((ITERS, 2 * RHS, RANK), f32),
        V((ITERS, N_SIB, 2 * RHS, RANK), f32),
        V((ITERS, N_SIB, 2 * ROWS, RANK), f32),
        V((ITERS, N_SIB - 1, 2 * ROWS, RANK), f32),
        V((PARENTS, 2 * ROWS, RANK), f32),
        V((PARENTS, 2 * ROWS, RANK), f32),
        V((ITERS, N_SIB, 2 * ROWS, RANK), f32),
        V((N_SIB, ROWS, 1, LEAF), f32),
        V((PARENTS, ROWS, LANES), f32),
        V((N_SIB, 1, LEAF), jnp.int32),
        V((N_SIB, ROWS, LEAF), f32),
        V((N_SIB, ROWS, LEAF), f32),
        pltpu.SMEM((1, NB_PAR), jnp.int32),
        D((13,)),
    ]
    peers = N_SIB - 1
    scratch += [D((ITERS, 14)), D((ITERS, N_SIB, 2))] + [D((ITERS, peers))] * 4
    scratch += [D((ITERS, N_Z - 1))] * 2 + [D((ITERS, N_Z))] * 2 + [D((ITERS, 2 * N_Z))] * 2
    scratch += [D((peers,))] * 6
    return pl.pallas_call(
        kernel,
        out_shape=(out, out),
        in_specs=specs,
        out_specs=(pl.BlockSpec(memory_space=pltpu.VMEM), pl.BlockSpec(memory_space=pltpu.VMEM)),
        scratch_shapes=scratch,
        compiler_params=pltpu.CompilerParams(
            collective_id=0, has_side_effects=True, vmem_limit_bytes=63 * 1024 * 1024
        ),
        name="richardson",
    )(*args)


def solution(mesh):
    placed = (
        P(None, "wide", "sib"),
        P("wide", "sib"),
        P(None, "wide", "sib"),
        P(None, "wide", "sib"),
        P("wide", "sib", None, None),
        P("wide", "sib", None, None),
        P("wide", "sib", None, None),
        P("wide", "sib", None, None),
        P("wide", "sib", None, None, None),
        P("wide", "sib", None, None, None),
        P("wide", None),
        P("wide", None, None, None),
        P("wide", None, None, None),
    )
    return jax.shard_map(
        body,
        mesh=mesh,
        in_specs=placed,
        out_specs=(P(None, "wide", "sib"), P(None, "wide", "sib")),
        check_vma=False,
    )
```

```python
import functools

import jax
import jax.numpy as jnp
from jax import lax
from jax.experimental import pallas as pl
from jax.experimental.pallas import tpu as pltpu
from jax.sharding import PartitionSpec as P

ITERS = 2
N_SIB = 8
N_Z = 8
LEAF = 512
RHS = 128
RANK = 256
NB_PAR = 4
PARENTS = 32
ROWS = RHS // N_SIB
LANES = 128

relax_step = 0.3
noise_level = 1.0

f32 = jnp.float32
bf16 = jnp.bfloat16
MESH = pl.DeviceIdType.MESH

SIB_ORDER = (1, 7, 4, 3, 5, 2, 6)
BLOCKS = ((1, 0), (0, -1), (0, 1), (1, -1), (1, 1), (0, 2), (1, 2))
Z_ORDER = (1, 7, 2, 6, 3, 5, 4)
TO_XLO = ((3, 3), (6, 1), (2, 1), (7, 1), (1, 1), (0, 1))
TO_CORE = ((3, 3), (6, 2), (1, 2), (0, 1))


def parts(v):
    high = v.astype(bf16)
    return high, (v - high.astype(f32)).astype(bf16)


def dot(left, right):
    return jnp.dot(left, right, preferred_element_type=f32)


def dot_t(left, right):
    return lax.dot_general(left, right, (((1,), (1,)), ((), ())), preferred_element_type=f32)


def product(left, right, op=dot):
    lh, ll = left
    rh, rl = right
    rows = lh.shape[0]
    both = op(jnp.concatenate([lh, ll], axis=0), rh)
    return both[:rows] + (both[rows:] + op(lh, rl))


def kernel(
    rhs_hbm, order_hbm, x_hbm, dx_hbm, dense_hbm, dense_d_hbm, basis_hbm, trans_hbm, sib_k_hbm, sib_d_hbm,
    partners_hbm, par_k_hbm, par_d_hbm,
    x_out, dx_out,
    x_in, dx_in, dense_in, dense_d_in, basis_in, trans_in, sib_k_in, sib_d_in, par_k_in, par_d_in,
    dense_h, dense_l, dense_d_h, dense_d_l, basis_h, basis_l, trans_h, trans_l,
    pair_h, pair_l, lift_h, lift_l, turn_h, turn_l,
    sib_k_h, sib_k_l, sib_d_h, sib_d_l, par_k_h, par_k_l, par_d_h, par_d_l,
    state, ahead, coeff, coeff_in, term, term_in, upper_0, upper_1, field,
    points_in, points, order, placed, rhs, partners,
    load_sem, coeff_s, coeff_r, term_s, term_r, field_s, field_r,
    z_s, z_r, xlo_s, xlo_r, core_s, core_r, rhs_s, rhs_r, order_s, order_r, back_s, back_r,
):
    me = lax.axis_index("sib")
    wide = lax.axis_index("wide")
    xlo, z, core = wide // 16, wide // 2 % N_Z, wide % 2

    def sib_at(o):
        return lax.rem(me + o, N_SIB)

    def sib_dev(o):
        return (sib_at(o), wide)

    xhi, y = me // 4, me % 4

    def near(dx, dy):
        return lax.rem(xhi + dx, 2) * 4 + lax.rem(y + dy + 4, 4)

    across, y_next, y_prev = (near(1, 0), wide), (near(0, 1), wide), (near(0, -1), wide)

    def parent(xl, zz, cc):
        return xl * 16 + lax.rem(zz + N_Z, N_Z) * 2 + cc

    loads = {}

    def load(name, src, dst, k):
        loads[name] = pltpu.make_async_copy(src, dst, load_sem.at[k])
        loads[name].start()

    load("x", x_hbm, x_in, 0)
    load("basis", basis_hbm.at[0, 0], basis_in, 1)
    load("dx", dx_hbm, dx_in, 2)
    load("trans", trans_hbm.at[0, 0], trans_in, 3)
    load("points", rhs_hbm.at[pl.ds(pl.multiple_of(me * ROWS, ROWS), ROWS)], points_in.at[me], 4)
    load("order", order_hbm, order.at[me], 5)
    load("dense", dense_hbm.at[0, 0], dense_in, 6)
    load("dense_d", dense_d_hbm.at[0, 0], dense_d_in, 7)
    load("partners", partners_hbm, partners, 12)
    load("par_k", par_k_hbm.at[0], par_k_in, 8)
    load("par_d", par_d_hbm.at[0], par_d_in, 9)
    load("sib_k", sib_k_hbm.at[0, 0], sib_k_in, 10)
    load("sib_d", sib_d_hbm.at[0, 0], sib_d_in, 11)

    barrier = pltpu.get_barrier_semaphore()

    def greet(device):
        pl.semaphore_signal(barrier, inc=1, device_id=device, device_id_type=MESH)

    for o in range(1, N_SIB):
        greet(sib_dev(o))
    for d in range(1, N_Z):
        greet((me, parent(xlo, z + d, core)))
    greet((me, parent(1 - xlo, z, core)))
    greet((me, parent(xlo, z, 1 - core)))

    sent = []

    def send(src, dst, ssem, rsem, device):
        c = pltpu.make_async_remote_copy(
            src_ref=src, dst_ref=dst, send_sem=ssem, recv_sem=rsem, device_id=device, device_id_type=MESH
        )
        c.start()
        sent.append(c)
        return c

    def arrived(buf, sem):
        pltpu.make_async_copy(buf, buf, sem).wait()

    def slot(dx, dy):
        return dx % 2 * 4 + dy % 4

    def split(src, high, low):
        h, l = parts(src)
        high[...] = h
        low[...] = l

    def coefficients(it):
        v = parts(state[it])
        c = product(v, (basis_h[...], basis_l[...]))
        keep(it, c, product(parts(c), (trans_h[...], trans_l[...])))

    def keep(it, c, t):
        coeff[it] = c
        for s in range(N_SIB):
            term[it, s, :ROWS] = t[s * ROWS:(s + 1) * ROWS]
            term[it, s, ROWS:] = t[RHS + s * ROWS:RHS + (s + 1) * ROWS]

    loads["x"].wait()
    state[0, :RHS] = x_in[...].reshape(RHS, LEAF)
    loads["basis"].wait()
    split(basis_in[...], basis_h, basis_l)
    loads["dx"].wait()
    state[0, RHS:] = dx_in[...].reshape(RHS, LEAF)
    loads["trans"].wait()
    split(trans_in[...], trans_h, trans_l)
    coefficients(0)

    pl.semaphore_wait(barrier, 7 + 7 + 2)

    for it in range(ITERS):
        last = it == ITERS - 1
        upper = (upper_0, upper_1)[it]
        for o in SIB_ORDER:
            send(term.at[it, sib_at(o)], term_in.at[it, o - 1], term_s.at[it, o - 1], term_r.at[it, o - 1], sib_dev(o))
        if it == 0:
            loads["points"].wait()
            loads["order"].wait()
            for o in SIB_ORDER:
                send(order.at[me], order.at[me], order_s.at[o - 1], order_r.at[o - 1], sib_dev(o))
                send(
                    rhs_hbm.at[pl.ds(pl.multiple_of(sib_at(o) * ROWS, ROWS), ROWS)], points_in.at[me],
                    rhs_s.at[o - 1], rhs_r.at[o - 1], sib_dev(o),
                )
        gathered = []

        def piece(dx, dy, half):
            return coeff_in.at[it, slot(dx, dy), pl.ds(half * RHS, RHS)]

        def pass_on(src, dx, dy, half, device):
            send(src, piece(dx, dy, half), coeff_s.at[it, len(gathered)], coeff_r.at[it, slot(dx, dy), half], device)
            gathered.append(None)

        def have(dx, dy, half):
            arrived(piece(dx, dy, half), coeff_r.at[it, slot(dx, dy), half])

        for half in range(2):
            mine = coeff.at[it, pl.ds(half * RHS, RHS)]
            pass_on(mine, 1, 0, half, across)
            pass_on(mine, 0, -1, half, y_next)
            pass_on(mine, 0, 1, half, y_prev)

        if it == 0:
            loads["dense"].wait()
            split(dense_in[...], dense_h, dense_l)
            loads["dense_d"].wait()
            split(dense_d_in[...], dense_d_h, dense_d_l)
            loads["par_k"].wait()
            split(par_k_in[...], par_k_h, par_k_l)
            loads["par_d"].wait()
            split(par_d_in[...], par_d_h, par_d_l)
        else:
            state[it] = ahead[...] - relax_step * product(field_parts, (lift_h[...], lift_l[...]))
        v = state[it]
        vh, vl = parts(v)
        own = product((vh, vl), (dense_h[...], dense_l[...]))
        own_d = product((vh[:RHS], vl[:RHS]), (dense_d_h[...], dense_d_l[...]))
        ahead[:RHS] = v[:RHS] - relax_step * (noise_level * v[:RHS] + own[:RHS])
        ahead[RHS:] = v[RHS:] - relax_step * (noise_level * v[RHS:] + (own[RHS:] + own_d))

        total = term[it, me]
        for o in SIB_ORDER:
            arrived(term_in.at[it, o - 1], term_r.at[it, o - 1])
            total = total + term_in[it, o - 1]
        upper[core, xlo, 4] = total

        for d in Z_ORDER:
            send(
                upper.at[core, xlo, 4], upper.at[core, xlo, (d + 4) % N_Z], z_s.at[it, d - 1], z_r.at[it, d - 1],
                (me, parent(xlo, z + d, core)),
            )

        def to_xlo(k):
            run = upper.at[core, xlo, pl.ds(*TO_XLO[k])]
            send(run, run, xlo_s.at[it, k], xlo_r.at[it, k], (me, parent(1 - xlo, z, core)))

        def to_core(far, k):
            run = upper.at[core, far + xlo - 2 * far * xlo, pl.ds(*TO_CORE[k])]
            send(run, run, core_s.at[it, far, k], core_r.at[it, far, k], (me, parent(xlo, z, 1 - core)))

        def from_z(d):
            arrived(upper.at[core, xlo, (d + 4) % N_Z], z_r.at[it, d - 1])

        def from_xlo(k):
            arrived(upper.at[core, 1 - xlo, pl.ds(*TO_XLO[k])], xlo_r.at[it, k])

        def from_core(far, k):
            arrived(upper.at[1 - core, far + xlo - 2 * far * xlo, pl.ds(*TO_CORE[k])], core_r.at[it, far, k])

        def onward(half):
            have(1, 0, half)
            pass_on(piece(1, 0, half), 1, -1, half, y_next)
            pass_on(piece(1, 0, half), 1, 1, half, y_prev)

        def opposite(dx):
            have(dx, -1, 0)
            pass_on(piece(dx, -1, 0), dx, 2, 0, y_next)
            have(dx, 1, 1)
            pass_on(piece(dx, 1, 1), dx, 2, 1, y_prev)

        def points_here():
            for o in SIB_ORDER:
                arrived(order.at[sib_at(o)], order_r.at[N_SIB - o - 1])
                arrived(points_in.at[sib_at(o)], rhs_r.at[N_SIB - o - 1])
            for s in range(N_SIB):
                seg = points_in[s].reshape(ROWS, LEAF)
                for q in range(LEAF // LANES):
                    points[s * (LEAF // LANES) + q] = seg[:, q * LANES:(q + 1) * LANES]

        def place(s, _):
            want_all = order[s]
            for q in range(LEAF // LANES):
                want = jnp.broadcast_to(want_all[:, q * LANES:(q + 1) * LANES], (ROWS, LANES))
                block = want // LANES
                lane = want % LANES
                got = jnp.zeros((ROWS, LANES), f32)
                for b in range(PARENTS):
                    found = jnp.take_along_axis(points[b], lane, axis=1, mode="promise_in_bounds")
                    got = jnp.where(block == b, found, got)
                placed[s, :, q * LANES:(q + 1) * LANES] = got
            return 0

        def place_two(k):
            if it == 0:
                lax.fori_loop(2 * k, 2 * k + 2, place, 0)

        def split_sib(first, end):
            if it == 0:
                for k in range(first, end):
                    split(sib_k_in[k], sib_k_h.at[k], sib_k_l.at[k])
                    split(sib_d_in[k], sib_d_h.at[k], sib_d_l.at[k])

        onward(0)
        onward(1)
        if it == 0:
            loads["sib_k"].wait()
            loads["sib_d"].wait()
        split_sib(0, 2)
        from_z(1)
        from_z(7)
        to_xlo(0)
        to_core(0, 0)
        if it == 0:
            points_here()
        from_z(2)
        to_xlo(1)
        from_z(6)
        to_xlo(2)
        place_two(0)
        from_xlo(0)
        to_core(1, 0)
        opposite(0)
        from_z(3)
        to_xlo(3)
        to_core(0, 1)
        place_two(1)
        from_z(5)
        to_xlo(4)
        to_core(0, 2)
        place_two(2)
        from_z(4)
        to_xlo(5)
        to_core(0, 3)
        opposite(1)
        from_xlo(1)
        from_xlo(3)
        to_core(1, 1)
        place_two(3)
        if it == 0:
            rhs[me] = placed[me]
            for o in SIB_ORDER:
                send(placed.at[sib_at(o)], rhs.at[me], back_s.at[o - 1], back_r.at[o - 1], sib_dev(o))
        from_xlo(2)
        from_xlo(4)
        to_core(1, 2)
        from_xlo(5)
        to_core(1, 3)
        split_sib(2, N_SIB - 1)
        if it == 0:
            loads["partners"].wait()
        for far in range(2):
            for k in range(len(TO_CORE)):
                from_core(far, k)

        hx = jnp.zeros((ROWS, RANK), f32)
        hd = jnp.zeros((ROWS, RANK), f32)
        for k in range(NB_PAR):
            who = partners[0, k]
            found = upper[who % 2, who // 16, lax.rem(z - who // 2 % N_Z + N_Z + 4, N_Z)]
            ch, cl = parts(found)
            kk = product((ch, cl), (par_k_h[k], par_k_l[k]))
            kd = product((ch[:ROWS], cl[:ROWS]), (par_d_h[k], par_d_l[k]))
            hx = hx + kk[:ROWS]
            hd = hd + (kk[ROWS:] + kd)
        field[it, me, :ROWS] = hx
        field[it, me, ROWS:] = hd
        for o in SIB_ORDER:
            send(field.at[it, me], field.at[it, me], field_s.at[it, o - 1], field_r.at[it, o - 1], sib_dev(o))

        if it == 0:
            both = product((basis_h[...], basis_l[...]), (trans_h[...], trans_l[...]))
            split(jnp.concatenate([basis_in[...], both], axis=1), pair_h, pair_l)
            split(both.T, lift_h, lift_l)
            split(product((lift_h[...], lift_l[...]), (pair_h[...], pair_l[...])), turn_h, turn_l)

        gx = jnp.zeros((2 * RHS, RANK), f32)
        gd = jnp.zeros((RHS, RANK), f32)
        for dx, dy in BLOCKS:
            for half in range(2):
                if dy == 2 or dy == 1 and half == 0 or dy == -1 and half == 1:
                    have(dx, dy, half)
            at = lax.rem(near(dx, dy) - me + N_SIB, N_SIB) - 1
            ah, al = parts(coeff_in[it, slot(dx, dy)])
            gx = gx + product((ah, al), (sib_k_h[at], sib_k_l[at]))
            gd = gd + product((ah[:RHS], al[:RHS]), (sib_d_h[at], sib_d_l[at]))
        near_field = jnp.concatenate([gx[:RHS], gx[RHS:] + gd], axis=0)
        known = ahead[...] - relax_step * product(parts(near_field), (basis_h[...], basis_l[...]), dot_t)
        if it == 0:
            for o in SIB_ORDER:
                arrived(rhs.at[sib_at(o)], back_r.at[N_SIB - o - 1])
        ahead[:RHS] = known[:RHS] + relax_step * rhs[...].reshape(RHS, LEAF)
        ahead[RHS:] = known[RHS:]
        if not last:
            known_c = product(parts(ahead[...]), (pair_h[...], pair_l[...]))

        for o in SIB_ORDER:
            arrived(field.at[it, sib_at(o)], field_r.at[it, N_SIB - o - 1])
        h = jnp.concatenate(
            [field[it, :, :ROWS].reshape(RHS, RANK), field[it, :, ROWS:].reshape(RHS, RANK)], axis=0
        )
        field_parts = parts(h)
        if last:
            result = ahead[...] - relax_step * product(field_parts, (lift_h[...], lift_l[...]))
            x_out[...] = result[:RHS].reshape(RHS, 1, LEAF)
            dx_out[...] = result[RHS:].reshape(RHS, 1, LEAF)
        else:
            next_c = known_c - relax_step * product(field_parts, (turn_h[...], turn_l[...]))
            keep(it + 1, next_c[:, :RANK], next_c[:, RANK:])

    for c in sent:
        c.wait_send()


def hand_on(x, dx, x_out, dx_out):
    x_out[...] = x[...]
    dx_out[...] = dx[...]


def body(*args):
    V = pltpu.VMEM
    D = pltpu.SemaphoreType.DMA
    specs = [pl.BlockSpec(memory_space=pltpu.HBM)] * 13
    out = jax.ShapeDtypeStruct((RHS, 1, LEAF), f32)
    weights = [(LEAF, LEAF)] * 2 + [(LEAF, RANK), (RANK, RANK)] + [(N_SIB - 1, RANK, RANK)] * 2 + [(NB_PAR, RANK, RANK)] * 2
    scratch = [V((RHS, 1, LEAF), f32)] * 2
    scratch += [V(w, f32) for w in weights]
    for w in weights[:4] + [(LEAF, 2 * RANK), (RANK, LEAF), (RANK, 2 * RANK)] + weights[4:]:
        scratch += [V(w, bf16)] * 2
    scratch += [
        V((ITERS, 2 * RHS, LEAF), f32),
        V((2 * RHS, LEAF), f32),
        V((ITERS, 2 * RHS, RANK), f32),
        V((ITERS, N_SIB, 2 * RHS, RANK), f32),
        V((ITERS, N_SIB, 2 * ROWS, RANK), f32),
        V((ITERS, N_SIB - 1, 2 * ROWS, RANK), f32),
        V((2, 2, N_Z, 2 * ROWS, RANK), f32),
        V((2, 2, N_Z, 2 * ROWS, RANK), f32),
        V((ITERS, N_SIB, 2 * ROWS, RANK), f32),
        V((N_SIB, ROWS, 1, LEAF), f32),
        V((PARENTS, ROWS, LANES), f32),
        V((N_SIB, 1, LEAF), jnp.int32),
        V((N_SIB, ROWS, LEAF), f32),
        V((N_SIB, ROWS, LEAF), f32),
        pltpu.SMEM((1, NB_PAR), jnp.int32),
        D((13,)),
    ]
    peers = N_SIB - 1
    scratch += [D((ITERS, 14)), D((ITERS, N_SIB, 2))] + [D((ITERS, peers))] * 4
    scratch += [D((ITERS, N_Z - 1))] * 2 + [D((ITERS, len(TO_XLO)))] * 2 + [D((ITERS, 2, len(TO_CORE)))] * 2
    scratch += [D((peers,))] * 6
    found = pl.pallas_call(
        kernel,
        out_shape=(out, out),
        in_specs=specs,
        out_specs=(pl.BlockSpec(memory_space=pltpu.VMEM), pl.BlockSpec(memory_space=pltpu.VMEM)),
        scratch_shapes=scratch,
        compiler_params=pltpu.CompilerParams(
            collective_id=0, has_side_effects=True, vmem_limit_bytes=63 * 1024 * 1024
        ),
        name="richardson",
    )(*args)
    whole = pl.BlockSpec(memory_space=pltpu.VMEM)
    return pl.pallas_call(
        hand_on, out_shape=(out, out), in_specs=[whole] * 2, out_specs=(whole, whole), name="hand_on"
    )(*found)


def solution(mesh):
    placed = (
        P(None, "wide", "sib"),
        P("wide", "sib"),
        P(None, "wide", "sib"),
        P(None, "wide", "sib"),
        P("wide", "sib", None, None),
        P("wide", "sib", None, None),
        P("wide", "sib", None, None),
        P("wide", "sib", None, None),
        P("wide", "sib", None, None, None),
        P("wide", "sib", None, None, None),
        P("wide", None),
        P("wide", None, None, None),
        P("wide", None, None, None),
    )
    return jax.shard_map(
        body,
        mesh=mesh,
        in_specs=placed,
        out_specs=(P(None, "wide", "sib"), P(None, "wide", "sib")),
        check_vma=False,
    )
```

```python
import functools

import jax
import jax.numpy as jnp
from jax import lax
from jax.experimental import pallas as pl
from jax.experimental.pallas import tpu as pltpu
from jax.sharding import PartitionSpec as P

ITERS = 2
N_SIB = 8
N_Z = 8
LEAF = 512
RHS = 128
RANK = 256
NB_PAR = 4
PARENTS = 32
ROWS = RHS // N_SIB
LANES = 128

relax_step = 0.3
noise_level = 1.0

f32 = jnp.float32
bf16 = jnp.bfloat16
MESH = pl.DeviceIdType.MESH

SIB_ORDER = (1, 7, 4, 3, 5, 2, 6)
BLOCKS = ((1, 0), (0, -1), (0, 1), (1, -1), (1, 1), (0, 2), (1, 2))
Z_ORDER = (1, 7, 2, 6, 3, 5, 4)
TO_XLO = ((3, 3), (6, 1), (2, 1), (7, 1), (1, 1), (0, 1))
TO_CORE = ((3, 3), (6, 2), (1, 2), (0, 1))


def parts(v):
    high = v.astype(bf16)
    return high, (v - high.astype(f32)).astype(bf16)


def dot(left, right):
    return jnp.dot(left, right, preferred_element_type=f32)


def dot_t(left, right):
    return lax.dot_general(left, right, (((1,), (1,)), ((), ())), preferred_element_type=f32)


def product(left, right, op=dot):
    lh, ll = left
    rh, rl = right
    rows = lh.shape[0]
    both = op(jnp.concatenate([lh, ll], axis=0), rh)
    return both[:rows] + (both[rows:] + op(lh, rl))


def kernel(
    rhs_hbm, order_hbm, x_hbm, dx_hbm, dense_hbm, dense_d_hbm, basis_hbm, trans_hbm, sib_k_hbm, sib_d_hbm,
    partners_hbm, par_k_hbm, par_d_hbm,
    x_out, dx_out,
    x_in, dx_in, dense_in, dense_d_in, basis_in, trans_in, sib_k_in, sib_d_in, par_k_in, par_d_in,
    dense_h, dense_l, dense_d_h, dense_d_l, basis_h, basis_l, trans_h, trans_l,
    pair_h, pair_l, lift_h, lift_l, turn_h, turn_l,
    sib_k_h, sib_k_l, sib_d_h, sib_d_l, par_k_h, par_k_l, par_d_h, par_d_l,
    state, ahead, coeff, coeff_in, term, term_in, upper_0, upper_1, field,
    points_in, points, order, placed, rhs, partners,
    load_sem, coeff_s, coeff_r, term_s, term_r, field_s, field_r,
    z_s, z_r, xlo_s, xlo_r, core_s, core_r, rhs_s, rhs_r, order_s, order_r, back_s, back_r,
):
    me = lax.axis_index("sib")
    wide = lax.axis_index("wide")
    xlo, z, core = wide // 16, wide // 2 % N_Z, wide % 2

    def sib_at(o):
        return lax.rem(me + o, N_SIB)

    def sib_dev(o):
        return (sib_at(o), wide)

    xhi, y = me // 4, me % 4

    def near(dx, dy):
        return lax.rem(xhi + dx, 2) * 4 + lax.rem(y + dy + 4, 4)

    across, y_next, y_prev = (near(1, 0), wide), (near(0, 1), wide), (near(0, -1), wide)

    def parent(xl, zz, cc):
        return xl * 16 + lax.rem(zz + N_Z, N_Z) * 2 + cc

    loads = {}

    def load(name, src, dst, k):
        loads[name] = pltpu.make_async_copy(src, dst, load_sem.at[k])
        loads[name].start()

    load("x", x_hbm, x_in, 0)
    load("basis", basis_hbm.at[0, 0], basis_in, 1)
    load("dx", dx_hbm, dx_in, 2)
    load("trans", trans_hbm.at[0, 0], trans_in, 3)
    load("points", rhs_hbm.at[pl.ds(pl.multiple_of(me * ROWS, ROWS), ROWS)], points_in.at[me], 4)
    load("order", order_hbm, order.at[me], 5)

    barrier = pltpu.get_barrier_semaphore()

    def greet(device):
        pl.semaphore_signal(barrier, inc=1, device_id=device, device_id_type=MESH)

    for o in range(1, N_SIB):
        greet(sib_dev(o))
    for d in range(1, N_Z):
        greet((me, parent(xlo, z + d, core)))
    greet((me, parent(1 - xlo, z, core)))
    greet((me, parent(xlo, z, 1 - core)))

    sent = []

    def send(src, dst, ssem, rsem, device):
        c = pltpu.make_async_remote_copy(
            src_ref=src, dst_ref=dst, send_sem=ssem, recv_sem=rsem, device_id=device, device_id_type=MESH
        )
        c.start()
        sent.append(c)
        return c

    def arrived(buf, sem):
        pltpu.make_async_copy(buf, buf, sem).wait()

    def slot(dx, dy):
        return dx % 2 * 4 + dy % 4

    def split(src, high, low):
        h, l = parts(src)
        high[...] = h
        low[...] = l

    def coefficients(it):
        v = parts(state[it])
        c = product(v, (basis_h[...], basis_l[...]))
        keep(it, c, product(parts(c), (trans_h[...], trans_l[...])))

    def keep(it, c, t):
        coeff[it] = c
        for s in range(N_SIB):
            term[it, s, :ROWS] = t[s * ROWS:(s + 1) * ROWS]
            term[it, s, ROWS:] = t[RHS + s * ROWS:RHS + (s + 1) * ROWS]

    loads["x"].wait()
    state[0, :RHS] = x_in[...].reshape(RHS, LEAF)
    loads["basis"].wait()
    split(basis_in[...], basis_h, basis_l)
    loads["dx"].wait()
    state[0, RHS:] = dx_in[...].reshape(RHS, LEAF)
    loads["trans"].wait()
    load("dense", dense_hbm.at[0, 0], dense_in, 6)
    load("dense_d", dense_d_hbm.at[0, 0], dense_d_in, 7)
    load("partners", partners_hbm, partners, 12)
    load("par_k", par_k_hbm.at[0], par_k_in, 8)
    load("par_d", par_d_hbm.at[0], par_d_in, 9)
    load("sib_k", sib_k_hbm.at[0, 0], sib_k_in, 10)
    load("sib_d", sib_d_hbm.at[0, 0], sib_d_in, 11)
    split(trans_in[...], trans_h, trans_l)
    coefficients(0)

    pl.semaphore_wait(barrier, 7 + 7 + 2)

    for it in range(ITERS):
        last = it == ITERS - 1
        upper = (upper_0, upper_1)[it]
        for o in SIB_ORDER:
            send(term.at[it, sib_at(o)], term_in.at[it, o - 1], term_s.at[it, o - 1], term_r.at[it, o - 1], sib_dev(o))
        gathered = []

        def piece(dx, dy, half):
            return coeff_in.at[it, slot(dx, dy), pl.ds(half * RHS, RHS)]

        def pass_on(src, dx, dy, half, device):
            send(src, piece(dx, dy, half), coeff_s.at[it, len(gathered)], coeff_r.at[it, slot(dx, dy), half], device)
            gathered.append(None)

        def have(dx, dy, half):
            arrived(piece(dx, dy, half), coeff_r.at[it, slot(dx, dy), half])

        for half in range(2):
            mine = coeff.at[it, pl.ds(half * RHS, RHS)]
            pass_on(mine, 1, 0, half, across)
            pass_on(mine, 0, -1, half, y_next)
            pass_on(mine, 0, 1, half, y_prev)

        if it == 0:
            loads["dense"].wait()
            split(dense_in[...], dense_h, dense_l)
            loads["dense_d"].wait()
            split(dense_d_in[...], dense_d_h, dense_d_l)
            loads["par_k"].wait()
            split(par_k_in[...], par_k_h, par_k_l)
            loads["par_d"].wait()
            split(par_d_in[...], par_d_h, par_d_l)
        else:
            state[it] = ahead[...] - relax_step * product(field_parts, (lift_h[...], lift_l[...]))
        v = state[it]
        vh, vl = parts(v)
        own = product((vh, vl), (dense_h[...], dense_l[...]))
        own_d = product((vh[:RHS], vl[:RHS]), (dense_d_h[...], dense_d_l[...]))
        ahead[:RHS] = v[:RHS] - relax_step * (noise_level * v[:RHS] + own[:RHS])
        ahead[RHS:] = v[RHS:] - relax_step * (noise_level * v[RHS:] + (own[RHS:] + own_d))

        total = term[it, me]
        for o in SIB_ORDER:
            arrived(term_in.at[it, o - 1], term_r.at[it, o - 1])
            total = total + term_in[it, o - 1]
        upper[core, xlo, 4] = total

        for d in Z_ORDER:
            send(
                upper.at[core, xlo, 4], upper.at[core, xlo, (d + 4) % N_Z], z_s.at[it, d - 1], z_r.at[it, d - 1],
                (me, parent(xlo, z + d, core)),
            )

        if it == 0:
            loads["points"].wait()
            loads["order"].wait()
            for o in SIB_ORDER:
                send(order.at[me], order.at[me], order_s.at[o - 1], order_r.at[o - 1], sib_dev(o))
                send(
                    rhs_hbm.at[pl.ds(pl.multiple_of(sib_at(o) * ROWS, ROWS), ROWS)], points_in.at[me],
                    rhs_s.at[o - 1], rhs_r.at[o - 1], sib_dev(o),
                )
        def to_xlo(k):
            run = upper.at[core, xlo, pl.ds(*TO_XLO[k])]
            send(run, run, xlo_s.at[it, k], xlo_r.at[it, k], (me, parent(1 - xlo, z, core)))

        def to_core(far, k):
            run = upper.at[core, far + xlo - 2 * far * xlo, pl.ds(*TO_CORE[k])]
            send(run, run, core_s.at[it, far, k], core_r.at[it, far, k], (me, parent(xlo, z, 1 - core)))

        def from_z(d):
            arrived(upper.at[core, xlo, (d + 4) % N_Z], z_r.at[it, d - 1])

        def from_xlo(k):
            arrived(upper.at[core, 1 - xlo, pl.ds(*TO_XLO[k])], xlo_r.at[it, k])

        def from_core(far, k):
            arrived(upper.at[1 - core, far + xlo - 2 * far * xlo, pl.ds(*TO_CORE[k])], core_r.at[it, far, k])

        def onward(half):
            have(1, 0, half)
            pass_on(piece(1, 0, half), 1, -1, half, y_next)
            pass_on(piece(1, 0, half), 1, 1, half, y_prev)

        def opposite(dx):
            have(dx, -1, 0)
            pass_on(piece(dx, -1, 0), dx, 2, 0, y_next)
            have(dx, 1, 1)
            pass_on(piece(dx, 1, 1), dx, 2, 1, y_prev)

        def points_here():
            for o in SIB_ORDER:
                arrived(order.at[sib_at(o)], order_r.at[N_SIB - o - 1])
                arrived(points_in.at[sib_at(o)], rhs_r.at[N_SIB - o - 1])
            for s in range(N_SIB):
                seg = points_in[s].reshape(ROWS, LEAF)
                for q in range(LEAF // LANES):
                    points[s * (LEAF // LANES) + q] = seg[:, q * LANES:(q + 1) * LANES]

        def place(s, _):
            want_all = order[s]
            for q in range(LEAF // LANES):
                want = jnp.broadcast_to(want_all[:, q * LANES:(q + 1) * LANES], (ROWS, LANES))
                block = want // LANES
                lane = want % LANES
                got = jnp.zeros((ROWS, LANES), f32)
                for b in range(PARENTS):
                    found = jnp.take_along_axis(points[b], lane, axis=1, mode="promise_in_bounds")
                    got = jnp.where(block == b, found, got)
                placed[s, :, q * LANES:(q + 1) * LANES] = got
            return 0

        def place_two(k):
            if it == 0:
                lax.fori_loop(2 * k, 2 * k + 2, place, 0)

        def split_sib(first, end):
            if it == 0:
                for k in range(first, end):
                    split(sib_k_in[k], sib_k_h.at[k], sib_k_l.at[k])
                    split(sib_d_in[k], sib_d_h.at[k], sib_d_l.at[k])

        onward(0)
        onward(1)
        if it == 0:
            loads["sib_k"].wait()
            loads["sib_d"].wait()
        split_sib(0, N_SIB - 1)
        if it == 0:
            both = product((basis_h[...], basis_l[...]), (trans_h[...], trans_l[...]))
            split(jnp.concatenate([basis_in[...], both], axis=1), pair_h, pair_l)
            split(both.T, lift_h, lift_l)
            split(product((lift_h[...], lift_l[...]), (pair_h[...], pair_l[...])), turn_h, turn_l)

        opposite(0)
        from_z(1)
        from_z(7)
        to_xlo(0)
        to_core(0, 0)
        from_z(2)
        to_xlo(1)
        from_z(6)
        to_xlo(2)
        from_z(3)
        to_xlo(3)
        to_core(0, 1)
        from_z(5)
        to_xlo(4)
        to_core(0, 2)
        from_z(4)
        to_xlo(5)
        to_core(0, 3)
        if it == 0:
            points_here()
        place_two(0)
        from_xlo(0)
        to_core(1, 0)
        place_two(1)
        from_xlo(1)
        from_xlo(3)
        to_core(1, 1)
        place_two(2)
        opposite(1)
        from_xlo(2)
        from_xlo(4)
        to_core(1, 2)
        place_two(3)
        if it == 0:
            rhs[me] = placed[me]
            for o in SIB_ORDER:
                send(placed.at[sib_at(o)], rhs.at[me], back_s.at[o - 1], back_r.at[o - 1], sib_dev(o))
        from_xlo(5)
        to_core(1, 3)
        if it == 0:
            loads["partners"].wait()
        for far in range(2):
            for k in range(len(TO_CORE)):
                from_core(far, k)

        hx = jnp.zeros((ROWS, RANK), f32)
        hd = jnp.zeros((ROWS, RANK), f32)
        for k in range(NB_PAR):
            who = partners[0, k]
            found = upper[who % 2, who // 16, lax.rem(z - who // 2 % N_Z + N_Z + 4, N_Z)]
            ch, cl = parts(found)
            kk = product((ch, cl), (par_k_h[k], par_k_l[k]))
            kd = product((ch[:ROWS], cl[:ROWS]), (par_d_h[k], par_d_l[k]))
            hx = hx + kk[:ROWS]
            hd = hd + (kk[ROWS:] + kd)
        field[it, me, :ROWS] = hx
        field[it, me, ROWS:] = hd
        for o in SIB_ORDER:
            send(field.at[it, me], field.at[it, me], field_s.at[it, o - 1], field_r.at[it, o - 1], sib_dev(o))

        gx = jnp.zeros((2 * RHS, RANK), f32)
        gd = jnp.zeros((RHS, RANK), f32)
        for dx, dy in BLOCKS:
            for half in range(2):
                if dy == 2 or dy == 1 and half == 0 or dy == -1 and half == 1:
                    have(dx, dy, half)
            at = lax.rem(near(dx, dy) - me + N_SIB, N_SIB) - 1
            ah, al = parts(coeff_in[it, slot(dx, dy)])
            gx = gx + product((ah, al), (sib_k_h[at], sib_k_l[at]))
            gd = gd + product((ah[:RHS], al[:RHS]), (sib_d_h[at], sib_d_l[at]))
        near_field = jnp.concatenate([gx[:RHS], gx[RHS:] + gd], axis=0)
        known = ahead[...] - relax_step * product(parts(near_field), (basis_h[...], basis_l[...]), dot_t)
        if it == 0:
            for o in SIB_ORDER:
                arrived(rhs.at[sib_at(o)], back_r.at[N_SIB - o - 1])
        ahead[:RHS] = known[:RHS] + relax_step * rhs[...].reshape(RHS, LEAF)
        ahead[RHS:] = known[RHS:]
        if not last:
            known_c = product(parts(ahead[...]), (pair_h[...], pair_l[...]))

        for o in SIB_ORDER:
            arrived(field.at[it, sib_at(o)], field_r.at[it, N_SIB - o - 1])
        h = jnp.concatenate(
            [field[it, :, :ROWS].reshape(RHS, RANK), field[it, :, ROWS:].reshape(RHS, RANK)], axis=0
        )
        field_parts = parts(h)
        if last:
            result = ahead[...] - relax_step * product(field_parts, (lift_h[...], lift_l[...]))
            x_out[...] = result[:RHS].reshape(RHS, 1, LEAF)
            dx_out[...] = result[RHS:].reshape(RHS, 1, LEAF)
        else:
            next_c = known_c - relax_step * product(field_parts, (turn_h[...], turn_l[...]))
            keep(it + 1, next_c[:, :RANK], next_c[:, RANK:])

    for c in sent:
        c.wait_send()


def hand_on(x, dx, x_out, dx_out):
    x_out[...] = x[...]
    dx_out[...] = dx[...]


def body(*args):
    V = pltpu.VMEM
    D = pltpu.SemaphoreType.DMA
    specs = [pl.BlockSpec(memory_space=pltpu.HBM)] * 13
    out = jax.ShapeDtypeStruct((RHS, 1, LEAF), f32)
    weights = [(LEAF, LEAF)] * 2 + [(LEAF, RANK), (RANK, RANK)] + [(N_SIB - 1, RANK, RANK)] * 2 + [(NB_PAR, RANK, RANK)] * 2
    scratch = [V((RHS, 1, LEAF), f32)] * 2
    scratch += [V(w, f32) for w in weights]
    for w in weights[:4] + [(LEAF, 2 * RANK), (RANK, LEAF), (RANK, 2 * RANK)] + weights[4:]:
        scratch += [V(w, bf16)] * 2
    scratch += [
        V((ITERS, 2 * RHS, LEAF), f32),
        V((2 * RHS, LEAF), f32),
        V((ITERS, 2 * RHS, RANK), f32),
        V((ITERS, N_SIB, 2 * RHS, RANK), f32),
        V((ITERS, N_SIB, 2 * ROWS, RANK), f32),
        V((ITERS, N_SIB - 1, 2 * ROWS, RANK), f32),
        V((2, 2, N_Z, 2 * ROWS, RANK), f32),
        V((2, 2, N_Z, 2 * ROWS, RANK), f32),
        V((ITERS, N_SIB, 2 * ROWS, RANK), f32),
        V((N_SIB, ROWS, 1, LEAF), f32),
        V((PARENTS, ROWS, LANES), f32),
        V((N_SIB, 1, LEAF), jnp.int32),
        V((N_SIB, ROWS, LEAF), f32),
        V((N_SIB, ROWS, LEAF), f32),
        pltpu.SMEM((1, NB_PAR), jnp.int32),
        D((13,)),
    ]
    peers = N_SIB - 1
    scratch += [D((ITERS, 14)), D((ITERS, N_SIB, 2))] + [D((ITERS, peers))] * 4
    scratch += [D((ITERS, N_Z - 1))] * 2 + [D((ITERS, len(TO_XLO)))] * 2 + [D((ITERS, 2, len(TO_CORE)))] * 2
    scratch += [D((peers,))] * 6
    found = pl.pallas_call(
        kernel,
        out_shape=(out, out),
        in_specs=specs,
        out_specs=(pl.BlockSpec(memory_space=pltpu.VMEM), pl.BlockSpec(memory_space=pltpu.VMEM)),
        scratch_shapes=scratch,
        compiler_params=pltpu.CompilerParams(
            collective_id=0, has_side_effects=True, vmem_limit_bytes=63 * 1024 * 1024
        ),
        name="richardson",
    )(*args)
    whole = pl.BlockSpec(memory_space=pltpu.VMEM)
    return pl.pallas_call(
        hand_on, out_shape=(out, out), in_specs=[whole] * 2, out_specs=(whole, whole), name="hand_on"
    )(*found)


def solution(mesh):
    placed = (
        P(None, "wide", "sib"),
        P("wide", "sib"),
        P(None, "wide", "sib"),
        P(None, "wide", "sib"),
        P("wide", "sib", None, None),
        P("wide", "sib", None, None),
        P("wide", "sib", None, None),
        P("wide", "sib", None, None),
        P("wide", "sib", None, None, None),
        P("wide", "sib", None, None, None),
        P("wide", None),
        P("wide", None, None, None),
        P("wide", None, None, None),
    )
    return jax.shard_map(
        body,
        mesh=mesh,
        in_specs=placed,
        out_specs=(P(None, "wide", "sib"), P(None, "wide", "sib")),
        check_vma=False,
    )
```

```python
import functools

import jax
import jax.numpy as jnp
from jax import lax
from jax.experimental import pallas as pl
from jax.experimental.pallas import tpu as pltpu
from jax.sharding import PartitionSpec as P

ITERS = 2
N_SIB = 8
N_Z = 8
LEAF = 512
RHS = 128
RANK = 256
NB_PAR = 4
PARENTS = 32
ROWS = RHS // N_SIB
LANES = 128

relax_step = 0.3
noise_level = 1.0

f32 = jnp.float32
bf16 = jnp.bfloat16
MESH = pl.DeviceIdType.MESH

SIB_ORDER = (1, 7, 4, 3, 5, 2, 6)
BLOCKS = ((1, 0), (0, -1), (0, 1), (1, -1), (1, 1), (0, 2), (1, 2))
Z_ORDER = (1, 7, 2, 6, 3, 5, 4)
TO_XLO = ((3, 3), (6, 1), (2, 1), (7, 1), (1, 1), (0, 1))
TO_CORE = ((3, 3), (6, 2), (1, 2), (0, 1))


def parts(v):
    high = v.astype(bf16)
    return high, (v - high.astype(f32)).astype(bf16)


def dot(left, right):
    return jnp.dot(left, right, preferred_element_type=f32)


def dot_t(left, right):
    return lax.dot_general(left, right, (((1,), (1,)), ((), ())), preferred_element_type=f32)


def product(left, right, op=dot):
    lh, ll = left
    rh, rl = right
    rows = lh.shape[0]
    both = op(jnp.concatenate([lh, ll], axis=0), rh)
    return both[:rows] + (both[rows:] + op(lh, rl))


def kernel(
    rhs_hbm, order_hbm, x_hbm, dx_hbm, dense_hbm, dense_d_hbm, basis_hbm, trans_hbm, sib_k_hbm, sib_d_hbm,
    partners_hbm, par_k_hbm, par_d_hbm,
    x_out, dx_out,
    x_in, dx_in, dense_in, dense_d_in, basis_in, trans_in, sib_k_in, sib_d_in, par_k_in, par_d_in,
    dense_h, dense_l, dense_d_h, dense_d_l, basis_h, basis_l, trans_h, trans_l,
    pair_h, pair_l, lift_h, lift_l, turn_h, turn_l,
    sib_k_h, sib_k_l, sib_d_h, sib_d_l, par_k_h, par_k_l, par_d_h, par_d_l,
    state, ahead, coeff, coeff_in, term, term_in, upper_0, upper_1, field,
    points_in, points, order, placed, rhs, partners,
    load_sem, coeff_s, coeff_r, term_s, term_r, field_s, field_r,
    z_s, z_r, xlo_s, xlo_r, core_s, core_r, rhs_s, rhs_r, order_s, order_r, back_s, back_r,
):
    me = lax.axis_index("sib")
    wide = lax.axis_index("wide")
    xlo, z, core = wide // 16, wide // 2 % N_Z, wide % 2

    def sib_at(o):
        return lax.rem(me + o, N_SIB)

    def sib_dev(o):
        return (sib_at(o), wide)

    xhi, y = me // 4, me % 4

    def near(dx, dy):
        return lax.rem(xhi + dx, 2) * 4 + lax.rem(y + dy + 4, 4)

    across, y_next, y_prev = (near(1, 0), wide), (near(0, 1), wide), (near(0, -1), wide)

    def parent(xl, zz, cc):
        return xl * 16 + lax.rem(zz + N_Z, N_Z) * 2 + cc

    loads = {}

    def load(name, src, dst, k):
        loads[name] = pltpu.make_async_copy(src, dst, load_sem.at[k])
        loads[name].start()

    load("x", x_hbm, x_in, 0)
    load("basis", basis_hbm.at[0, 0], basis_in, 1)
    load("dx", dx_hbm, dx_in, 2)
    load("trans", trans_hbm.at[0, 0], trans_in, 3)
    load("points", rhs_hbm.at[pl.ds(pl.multiple_of(me * ROWS, ROWS), ROWS)], points_in.at[me], 4)
    load("order", order_hbm, order.at[me], 5)

    barrier = pltpu.get_barrier_semaphore()

    def greet(device):
        pl.semaphore_signal(barrier, inc=1, device_id=device, device_id_type=MESH)

    for o in range(1, N_SIB):
        greet(sib_dev(o))
    for d in range(1, N_Z):
        greet((me, parent(xlo, z + d, core)))
    greet((me, parent(1 - xlo, z, core)))
    greet((me, parent(xlo, z, 1 - core)))

    sent = []

    def send(src, dst, ssem, rsem, device):
        c = pltpu.make_async_remote_copy(
            src_ref=src, dst_ref=dst, send_sem=ssem, recv_sem=rsem, device_id=device, device_id_type=MESH
        )
        c.start()
        sent.append(c)
        return c

    def arrived(buf, sem):
        pltpu.make_async_copy(buf, buf, sem).wait()

    def slot(dx, dy):
        return dx % 2 * 4 + dy % 4

    def split(src, high, low):
        h, l = parts(src)
        high[...] = h
        low[...] = l

    def coefficients(it):
        v = parts(state[it])
        c = product(v, (basis_h[...], basis_l[...]))
        keep(it, c, product(parts(c), (trans_h[...], trans_l[...])))

    def keep(it, c, t):
        coeff[it] = c
        for s in range(N_SIB):
            term[it, s, :ROWS] = t[s * ROWS:(s + 1) * ROWS]
            term[it, s, ROWS:] = t[RHS + s * ROWS:RHS + (s + 1) * ROWS]

    loads["x"].wait()
    state[0, :RHS] = x_in[...].reshape(RHS, LEAF)
    loads["basis"].wait()
    split(basis_in[...], basis_h, basis_l)
    loads["dx"].wait()
    state[0, RHS:] = dx_in[...].reshape(RHS, LEAF)
    loads["trans"].wait()
    load("dense", dense_hbm.at[0, 0], dense_in, 6)
    load("dense_d", dense_d_hbm.at[0, 0], dense_d_in, 7)
    load("partners", partners_hbm, partners, 12)
    load("par_k", par_k_hbm.at[0], par_k_in, 8)
    load("par_d", par_d_hbm.at[0], par_d_in, 9)
    load("sib_k", sib_k_hbm.at[0, 0], sib_k_in, 10)
    load("sib_d", sib_d_hbm.at[0, 0], sib_d_in, 11)
    split(trans_in[...], trans_h, trans_l)
    coefficients(0)

    pl.semaphore_wait(barrier, 7 + 7 + 2)

    for it in range(ITERS):
        last = it == ITERS - 1
        upper = (upper_0, upper_1)[it]
        for o in SIB_ORDER:
            send(term.at[it, sib_at(o)], term_in.at[it, o - 1], term_s.at[it, o - 1], term_r.at[it, o - 1], sib_dev(o))
        gathered = []

        def piece(dx, dy, half):
            return coeff_in.at[it, slot(dx, dy), pl.ds(half * RHS, RHS)]

        def pass_on(src, dx, dy, half, device):
            send(src, piece(dx, dy, half), coeff_s.at[it, len(gathered)], coeff_r.at[it, slot(dx, dy), half], device)
            gathered.append(None)

        def have(dx, dy, half):
            arrived(piece(dx, dy, half), coeff_r.at[it, slot(dx, dy), half])

        for half in range(2):
            mine = coeff.at[it, pl.ds(half * RHS, RHS)]
            pass_on(mine, 1, 0, half, across)
            pass_on(mine, 0, -1, half, y_next)
            pass_on(mine, 0, 1, half, y_prev)

        if it == 0:
            loads["dense"].wait()
            split(dense_in[...], dense_h, dense_l)
            loads["dense_d"].wait()
            split(dense_d_in[...], dense_d_h, dense_d_l)
            loads["par_k"].wait()
            split(par_k_in[...], par_k_h, par_k_l)
            loads["par_d"].wait()
            split(par_d_in[...], par_d_h, par_d_l)
        else:
            state[it] = ahead[...] - relax_step * product(field_parts, (lift_h[...], lift_l[...]))
        v = state[it]
        vh, vl = parts(v)
        own = product((vh, vl), (dense_h[...], dense_l[...]))
        own_d = product((vh[:RHS], vl[:RHS]), (dense_d_h[...], dense_d_l[...]))
        ahead[:RHS] = v[:RHS] - relax_step * (noise_level * v[:RHS] + own[:RHS])
        ahead[RHS:] = v[RHS:] - relax_step * (noise_level * v[RHS:] + (own[RHS:] + own_d))

        total = term[it, me]
        for o in SIB_ORDER:
            arrived(term_in.at[it, o - 1], term_r.at[it, o - 1])
            total = total + term_in[it, o - 1]
        upper[core, xlo, 4] = total

        for d in Z_ORDER:
            send(
                upper.at[core, xlo, 4], upper.at[core, xlo, (d + 4) % N_Z], z_s.at[it, d - 1], z_r.at[it, d - 1],
                (me, parent(xlo, z + d, core)),
            )

        if it == 0:
            loads["points"].wait()
            loads["order"].wait()
            for o in SIB_ORDER:
                send(order.at[me], order.at[me], order_s.at[o - 1], order_r.at[o - 1], sib_dev(o))
                send(
                    rhs_hbm.at[pl.ds(pl.multiple_of(sib_at(o) * ROWS, ROWS), ROWS)], points_in.at[me],
                    rhs_s.at[o - 1], rhs_r.at[o - 1], sib_dev(o),
                )
        def to_xlo(k):
            run = upper.at[core, xlo, pl.ds(*TO_XLO[k])]
            send(run, run, xlo_s.at[it, k], xlo_r.at[it, k], (me, parent(1 - xlo, z, core)))

        def to_core(far, k):
            run = upper.at[core, far + xlo - 2 * far * xlo, pl.ds(*TO_CORE[k])]
            send(run, run, core_s.at[it, far, k], core_r.at[it, far, k], (me, parent(xlo, z, 1 - core)))

        def from_z(d):
            arrived(upper.at[core, xlo, (d + 4) % N_Z], z_r.at[it, d - 1])

        def from_xlo(k):
            arrived(upper.at[core, 1 - xlo, pl.ds(*TO_XLO[k])], xlo_r.at[it, k])

        def from_core(far, k):
            arrived(upper.at[1 - core, far + xlo - 2 * far * xlo, pl.ds(*TO_CORE[k])], core_r.at[it, far, k])

        def onward(half):
            have(1, 0, half)
            pass_on(piece(1, 0, half), 1, -1, half, y_next)
            pass_on(piece(1, 0, half), 1, 1, half, y_prev)

        def opposite(dx):
            have(dx, -1, 0)
            pass_on(piece(dx, -1, 0), dx, 2, 0, y_next)
            have(dx, 1, 1)
            pass_on(piece(dx, 1, 1), dx, 2, 1, y_prev)

        def points_here():
            for o in SIB_ORDER:
                arrived(order.at[sib_at(o)], order_r.at[N_SIB - o - 1])
                arrived(points_in.at[sib_at(o)], rhs_r.at[N_SIB - o - 1])
            for s in range(N_SIB):
                seg = points_in[s].reshape(ROWS, LEAF)
                for q in range(LEAF // LANES):
                    points[s * (LEAF // LANES) + q] = seg[:, q * LANES:(q + 1) * LANES]

        def place(s, _):
            want_all = order[s]
            for q in range(LEAF // LANES):
                want = jnp.broadcast_to(want_all[:, q * LANES:(q + 1) * LANES], (ROWS, LANES))
                block = want // LANES
                lane = want % LANES
                got = jnp.zeros((ROWS, LANES), f32)
                for b in range(PARENTS):
                    found = jnp.take_along_axis(points[b], lane, axis=1, mode="promise_in_bounds")
                    got = jnp.where(block == b, found, got)
                placed[s, :, q * LANES:(q + 1) * LANES] = got
            return 0

        def place_two(k):
            if it == 0:
                lax.fori_loop(2 * k, 2 * k + 2, place, 0)

        def split_sib(first, end):
            if it == 0:
                for k in range(first, end):
                    split(sib_k_in[k], sib_k_h.at[k], sib_k_l.at[k])
                    split(sib_d_in[k], sib_d_h.at[k], sib_d_l.at[k])

        onward(0)
        onward(1)
        if it == 0:
            loads["sib_k"].wait()
            loads["sib_d"].wait()
        split_sib(0, N_SIB - 1)
        if it == 0:
            both = product((basis_h[...], basis_l[...]), (trans_h[...], trans_l[...]))
            split(jnp.concatenate([basis_in[...], both], axis=1), pair_h, pair_l)
            split(both.T, lift_h, lift_l)
            split(product((lift_h[...], lift_l[...]), (pair_h[...], pair_l[...])), turn_h, turn_l)

        opposite(0)
        from_z(1)
        from_z(7)
        to_xlo(0)
        to_core(0, 0)
        from_z(2)
        to_xlo(1)
        from_z(6)
        to_xlo(2)
        from_z(3)
        to_xlo(3)
        to_core(0, 1)
        from_z(5)
        to_xlo(4)
        to_core(0, 2)
        from_z(4)
        to_xlo(5)
        to_core(0, 3)
        if it == 0:
            points_here()
        place_two(0)
        from_xlo(0)
        to_core(1, 0)
        place_two(1)
        from_xlo(1)
        from_xlo(3)
        to_core(1, 1)
        place_two(2)
        opposite(1)
        from_xlo(2)
        from_xlo(4)
        to_core(1, 2)
        place_two(3)
        if it == 0:
            rhs[me] = placed[me]
            for o in SIB_ORDER:
                send(placed.at[sib_at(o)], rhs.at[me], back_s.at[o - 1], back_r.at[o - 1], sib_dev(o))
        from_xlo(5)
        to_core(1, 3)
        if it == 0:
            loads["partners"].wait()
        for far in range(2):
            for k in range(len(TO_CORE)):
                from_core(far, k)

        hx = jnp.zeros((ROWS, RANK), f32)
        hd = jnp.zeros((ROWS, RANK), f32)
        for k in range(NB_PAR):
            who = partners[0, k]
            found = upper[who % 2, who // 16, lax.rem(z - who // 2 % N_Z + N_Z + 4, N_Z)]
            ch, cl = parts(found)
            kk = product((ch, cl), (par_k_h[k], par_k_l[k]))
            kd = product((ch[:ROWS], cl[:ROWS]), (par_d_h[k], par_d_l[k]))
            hx = hx + kk[:ROWS]
            hd = hd + (kk[ROWS:] + kd)
        field[it, me, :ROWS] = hx
        field[it, me, ROWS:] = hd
        for o in SIB_ORDER:
            send(field.at[it, me], field.at[it, me], field_s.at[it, o - 1], field_r.at[it, o - 1], sib_dev(o))

        gx = jnp.zeros((2 * RHS, RANK), f32)
        gd = jnp.zeros((RHS, RANK), f32)
        for dx, dy in BLOCKS:
            for half in range(2):
                if dy == 2 or dy == 1 and half == 0 or dy == -1 and half == 1:
                    have(dx, dy, half)
            at = lax.rem(near(dx, dy) - me + N_SIB, N_SIB) - 1
            ah, al = parts(coeff_in[it, slot(dx, dy)])
            gx = gx + product((ah, al), (sib_k_h[at], sib_k_l[at]))
            gd = gd + product((ah[:RHS], al[:RHS]), (sib_d_h[at], sib_d_l[at]))
        near_field = jnp.concatenate([gx[:RHS], gx[RHS:] + gd], axis=0)
        known = ahead[...] - relax_step * product(parts(near_field), (basis_h[...], basis_l[...]), dot_t)
        if it == 0:
            for o in SIB_ORDER:
                arrived(rhs.at[sib_at(o)], back_r.at[N_SIB - o - 1])
        ahead[:RHS] = known[:RHS] + relax_step * rhs[...].reshape(RHS, LEAF)
        ahead[RHS:] = known[RHS:]
        if not last:
            known_c = product(parts(ahead[...]), (pair_h[...], pair_l[...]))

        if last:
            for c in sent[:-(N_SIB - 1)]:
                c.wait_send()
            del sent[:-(N_SIB - 1)]

        for o in SIB_ORDER:
            arrived(field.at[it, sib_at(o)], field_r.at[it, N_SIB - o - 1])
        h = jnp.concatenate(
            [field[it, :, :ROWS].reshape(RHS, RANK), field[it, :, ROWS:].reshape(RHS, RANK)], axis=0
        )
        field_parts = parts(h)
        if last:
            result = ahead[...] - relax_step * product(field_parts, (lift_h[...], lift_l[...]))
            x_out[...] = result[:RHS].reshape(RHS, 1, LEAF)
            dx_out[...] = result[RHS:].reshape(RHS, 1, LEAF)
        else:
            next_c = known_c - relax_step * product(field_parts, (turn_h[...], turn_l[...]))
            keep(it + 1, next_c[:, :RANK], next_c[:, RANK:])

    for c in sent:
        c.wait_send()


def hand_on(x, dx, x_out, dx_out):
    x_out[...] = x[...]
    dx_out[...] = dx[...]


def body(*args):
    V = pltpu.VMEM
    D = pltpu.SemaphoreType.DMA
    specs = [pl.BlockSpec(memory_space=pltpu.HBM)] * 13
    out = jax.ShapeDtypeStruct((RHS, 1, LEAF), f32)
    weights = [(LEAF, LEAF)] * 2 + [(LEAF, RANK), (RANK, RANK)] + [(N_SIB - 1, RANK, RANK)] * 2 + [(NB_PAR, RANK, RANK)] * 2
    scratch = [V((RHS, 1, LEAF), f32)] * 2
    scratch += [V(w, f32) for w in weights]
    for w in weights[:4] + [(LEAF, 2 * RANK), (RANK, LEAF), (RANK, 2 * RANK)] + weights[4:]:
        scratch += [V(w, bf16)] * 2
    scratch += [
        V((ITERS, 2 * RHS, LEAF), f32),
        V((2 * RHS, LEAF), f32),
        V((ITERS, 2 * RHS, RANK), f32),
        V((ITERS, N_SIB, 2 * RHS, RANK), f32),
        V((ITERS, N_SIB, 2 * ROWS, RANK), f32),
        V((ITERS, N_SIB - 1, 2 * ROWS, RANK), f32),
        V((2, 2, N_Z, 2 * ROWS, RANK), f32),
        V((2, 2, N_Z, 2 * ROWS, RANK), f32),
        V((ITERS, N_SIB, 2 * ROWS, RANK), f32),
        V((N_SIB, ROWS, 1, LEAF), f32),
        V((PARENTS, ROWS, LANES), f32),
        V((N_SIB, 1, LEAF), jnp.int32),
        V((N_SIB, ROWS, LEAF), f32),
        V((N_SIB, ROWS, LEAF), f32),
        pltpu.SMEM((1, NB_PAR), jnp.int32),
        D((13,)),
    ]
    peers = N_SIB - 1
    scratch += [D((ITERS, 14)), D((ITERS, N_SIB, 2))] + [D((ITERS, peers))] * 4
    scratch += [D((ITERS, N_Z - 1))] * 2 + [D((ITERS, len(TO_XLO)))] * 2 + [D((ITERS, 2, len(TO_CORE)))] * 2
    scratch += [D((peers,))] * 6
    found = pl.pallas_call(
        kernel,
        out_shape=(out, out),
        in_specs=specs,
        out_specs=(pl.BlockSpec(memory_space=pltpu.VMEM), pl.BlockSpec(memory_space=pltpu.VMEM)),
        scratch_shapes=scratch,
        compiler_params=pltpu.CompilerParams(
            collective_id=0, has_side_effects=True, vmem_limit_bytes=63 * 1024 * 1024
        ),
        name="richardson",
    )(*args)
    whole = pl.BlockSpec(memory_space=pltpu.VMEM)
    return pl.pallas_call(
        hand_on, out_shape=(out, out), in_specs=[whole] * 2, out_specs=(whole, whole), name="hand_on"
    )(*found)


def solution(mesh):
    placed = (
        P(None, "wide", "sib"),
        P("wide", "sib"),
        P(None, "wide", "sib"),
        P(None, "wide", "sib"),
        P("wide", "sib", None, None),
        P("wide", "sib", None, None),
        P("wide", "sib", None, None),
        P("wide", "sib", None, None),
        P("wide", "sib", None, None, None),
        P("wide", "sib", None, None, None),
        P("wide", None),
        P("wide", None, None, None),
        P("wide", None, None, None),
    )
    return jax.shard_map(
        body,
        mesh=mesh,
        in_specs=placed,
        out_specs=(P(None, "wide", "sib"), P(None, "wide", "sib")),
        check_vma=False,
    )
```
